32 devices in a mesh: slab: 8 (over z, core), brick: 4 (over y, x).
Axes of the slice: x: 2, y: 2, z: 4, core: 2. Of those that a mesh axis runs over, the one named last changes fastest.
Arguments:
- features: bfloat16 [64, 65536], P(None, ('slab', 'brick')), may hold values from -6 to 6
- tangents: bfloat16 [4, 64, 65536], P(None, None, ('slab', 'brick')), may hold values from -6 to 6
- route: int32 [65536, 1], P(('slab', 'brick')), may hold values from 0 to 3; in each aligned block of 2048 rows (0 to 2047, 2048 to 4095, ...) at most 1024 rows name the same one
- cell_local: int32 [65536], P(('slab', 'brick')), may hold values from 0 to 8191
- stencil: int32 [65536], P(('slab', 'brick')), may hold values from 0 to 7
- stencil_table: float32 [8, 64], replicated, may hold values from -6 to 6
- taps1: float32 [3, 3, 64], replicated, may hold values from -3.5 to 3.5
- taps2: float32 [3, 3, 64], replicated, may hold values from -3.5 to 3.5
- point1: bfloat16 [64, 64], replicated, may hold values from -0.75 to 0.75
- point2: bfloat16 [64, 64], replicated, may hold values from -0.75 to 0.75
- bias1: float32 [64], replicated, may hold values from -3 to 3
- bias2: float32 [64], replicated, may hold values from -3 to 3
- readout: float32 [64], replicated, may hold values from -12 to 12
Outputs:
- hvp: float32 [4, 64, 65536], P(None, None, ('slab', 'brick'))
The draws below stay inside these ranges and needn't reach their ends.
Inputs may be any that keep to these rules, and one draw needn't show every extreme that they name: `route`: at most 1024 of the atoms of one device name one brick, and some device names some brick exactly 1024 times.
All inputs are finite; a program needn't handle non-finite values.
Results may differ from the reference program's by a relative error of at most 0.008.
The reference program's roundings to bfloat16 on the way count: a program that leaves them out, or rounds other values in their place, can miss the bound.
Values may be sent and summed in bfloat16 or wider, within the bound.
No kernel may reach another device: no remote copies, remote signals or barrier semaphores. Data moves between devices by JAX's collectives and lax.ppermute only.
A program may use at most 192 MiB of HBM per device.

```python
import math
import jax
import jax.numpy as jnp
import numpy as np
from jax import lax

NG = 64
CH = 64
NT = 4
KSETS = 8
ATOM_DEV = 2048
CAP = 1024
CZ = 8
CY = 16
CELLS_DEV = 8192
ATOMS = 65536
N_BRICK = 4


def set_ends(entries, rng, low, top_value):
    extent = entries.shape
    index_at = [jax.random.randint(jax.random.fold_in(rng, axis), (), 0, extent[axis]) for axis in range(len(extent))]
    entries = entries.at[tuple(index_at)].set(low)
    longest = extent.index(max(extent))
    index_at[longest] = (index_at[longest] + 1) % extent[longest]
    return entries.at[tuple(index_at)].set(top_value)


def block_levels(own_key, extent, split, smallest, top_value):
    factor_of = 1.0
    for dim, shards_of in split:
        heights = jax.random.uniform(jax.random.fold_in(jax.random.fold_in(own_key, 6), dim), (shards_of,), jnp.float32, smallest / len(split), top_value / len(split))
        factor_of = factor_of * jnp.repeat(jnp.exp(heights), extent[dim] // shards_of).reshape((-1,) + (1,) * (len(extent) - 1 - dim))
    return factor_of


def deal_out(stream_key, own, number, rows, count, top, bound, skew):
    ranking = jax.random.permutation(stream_key, count)
    packed, usual = shares(count, rows * top, bound, skew, True), shares(count, rows * top, bound, skew, False)
    places = jnp.arange(count)

    def named(sizes, turn):
        used = int((sizes > 0).sum())
        fixed = max(1, used // 4)
        passed = fixed + (places - fixed + turn * (used - fixed)) % max(1, count - fixed)
        return jnp.zeros((count,), jnp.int32).at[ranking[jnp.where(places < fixed, places, passed)]].set(jnp.asarray(sizes, jnp.int32))

    sizes = jnp.where(number % 4 == 0, named(packed, number // 4), named(usual, number - number // 4 - 1))
    mixed = jax.random.permutation(jax.random.fold_in(own, 3), count)
    source_of, receiver = mixed[0:count // 2 * 2:2], mixed[1:count // 2 * 2:2]
    margin = jnp.minimum(sizes[source_of] - 1, bound - sizes[receiver]) // 2
    margin = jnp.where((source_of == ranking[0]) | (receiver == ranking[0]) | (sizes[receiver] == 0), 0, jnp.maximum(margin, 0))
    passed = jax.random.randint(jax.random.fold_in(own, 4), (count // 2,), 0, 1 << 20) % (margin + 1)
    sizes = sizes.at[source_of].add(-passed).at[receiver].add(passed)
    labels = jnp.searchsorted(jnp.cumsum(sizes), jnp.arange(rows * top), side="right").astype(jnp.int32)
    table = labels.reshape(top, rows).T
    table = table[jax.random.permutation(jax.random.fold_in(own, 1), rows)]
    turn = jax.random.randint(jax.random.fold_in(own, 2), (rows, 1), 0, top)
    return jnp.take_along_axis(table, (jnp.arange(top)[None, :] + turn) % top, axis=1)


def shares(amount, total, reach, skew, full):
    portions = [(1 << 20) // math.isqrt(grade ** skew) + 1 for grade in range(1, amount + 1)]
    largest = reach if full else min(reach, max(-(-total // amount), total * portions[0] // sum(portions)))
    least = 1 if total - largest >= amount - 1 else 0
    counts, rest = [largest] + [least] * (amount - 1), total - largest - least * (amount - 1)
    while rest > 0:
        movable = [i for i in range(1, amount) if counts[i] < largest] or [i for i in range(1, amount) if counts[i] < reach]
        pool, budget = sum([portions[i] for i in movable]), rest
        for i in movable:
            extra = min(reach - counts[i], max(1, budget * portions[i] // pool), rest)
            counts[i] = counts[i] + extra
            rest = rest - extra
    return np.array(counts)


def gaussian(own_key, dims, deviation, limit, split=(), kind=jnp.bfloat16):
    result = deviation * jax.random.normal(own_key, dims, jnp.float32)
    if split:
        result = result * block_levels(own_key, dims, split, -0.22, 0.18)
    return jnp.clip(result, -limit, limit).astype(kind)


def setup_inputs(seed: int = 0) -> dict:
    splits = jax.random.split(jax.random.key(seed), 14)
    features = gaussian(splits[0], (CH, ATOMS), 1.0, 6.0, ((1, 32),))
    tangents = gaussian(splits[1], (NT, CH, ATOMS), 1.0, 6.0, ((2, 32),))
    route_keys = jax.random.split(jax.random.fold_in(splits[2], 1), ATOMS // ATOM_DEV)
    route_turns = jax.random.permutation(jax.random.fold_in(splits[2], 3), ATOMS // ATOM_DEV)
    route = jax.vmap(lambda own, number: deal_out(jax.random.fold_in(splits[2], 2), own, number, ATOM_DEV, N_BRICK, 1, CAP, 2))(route_keys, route_turns).reshape((ATOMS, 1))
    cell_local = set_ends(jax.random.randint(splits[3], (ATOMS,), 0, CELLS_DEV), jax.random.fold_in(splits[3], 1), 0, CELLS_DEV - 1).astype(jnp.int32)
    stencil = set_ends(jax.random.randint(splits[4], (ATOMS,), 0, KSETS), jax.random.fold_in(splits[4], 1), 0, KSETS - 1).astype(jnp.int32)
    stencil_table = gaussian(splits[5], (KSETS, CH), 1.0, 6.0, (), jnp.float32)
    taps1 = gaussian(splits[6], (3, 3, CH), 0.6, 3.5, (), jnp.float32)
    taps2 = gaussian(splits[7], (3, 3, CH), 0.6, 3.5, (), jnp.float32)
    point1 = gaussian(splits[8], (CH, CH), CH ** -0.5, 0.75)
    point2 = gaussian(splits[9], (CH, CH), CH ** -0.5, 0.75)
    bias1 = gaussian(splits[10], (CH,), 0.5, 3.0, (), jnp.float32)
    bias2 = gaussian(splits[11], (CH,), 0.5, 3.0, (), jnp.float32)
    readout = gaussian(splits[12], (CH,), 2.0, 12.0, (), jnp.float32)
    return dict(features=features, tangents=tangents, route=route, cell_local=cell_local, stencil=stencil, stencil_table=stencil_table, taps1=taps1, taps2=taps2, point1=point1, point2=point2, bias1=bias1, bias2=bias2, readout=readout)


def dsilu(v):
    sg = jax.nn.sigmoid(v)
    return sg * (1.0 + v * (1.0 - sg))


def ddsilu(v):
    sg = jax.nn.sigmoid(v)
    return sg * (1.0 - sg) * (2.0 + v * (1.0 - 2.0 * sg))


def depth_ref(field, taps, flip):
    out = field.astype(jnp.float32)
    for axis in range(3):
        wts = taps[axis]
        if flip:
            wts = wts[::-1]
        lower = wts[0][:, None, None, None]
        middle = wts[1][:, None, None, None]
        upper = wts[2][:, None, None, None]
        out = lower * jnp.roll(out, 1, axis + 1) + middle * out + upper * jnp.roll(out, -1, axis + 1)
    return out


def mixing(point, field):
    return jnp.dot(point, field.reshape(CH, -1), preferred_element_type=jnp.float32).reshape(field.shape)


def reference(features, tangents, route, cell_local, stencil, stencil_table, taps1, taps2, point1, point2, bias1, bias2, readout):
    count_all = features.shape[1]
    index = jnp.arange(count_all, dtype=jnp.int32)
    slab_of = index // (N_BRICK * ATOM_DEV)
    brick_of = route[:, 0]
    z_part = cell_local // (CY * NG)
    y_part = (cell_local // NG) % CY
    x_part = cell_local % NG
    flat = ((slab_of * CZ + z_part) * NG + brick_of * CY + y_part) * NG + x_part
    tab = jnp.take(stencil_table, stencil, axis=0).T

    def deposit(values):
        dep = lax.optimization_barrier((values.astype(jnp.float32) * tab).astype(jnp.bfloat16))
        grid = jnp.zeros((CH, NG * NG * NG), jnp.float32).at[:, flat].add(dep.astype(jnp.float32))
        return grid.astype(jnp.bfloat16).reshape(CH, NG, NG, NG)

    bias_one = bias1[:, None, None, None]
    bias_two = bias2[:, None, None, None]
    scale = readout[:, None, None, None]
    charge = deposit(features)
    pre1 = mixing(point1, depth_ref(charge, taps1, False).astype(jnp.bfloat16)) + bias_one
    hidden = jax.nn.silu(pre1).astype(jnp.bfloat16)
    pre2 = mixing(point2, depth_ref(hidden, taps2, False).astype(jnp.bfloat16)) + bias_two
    g_two = (dsilu(pre2) * scale).astype(jnp.bfloat16)
    g_one = depth_ref(mixing(point2.T, g_two).astype(jnp.bfloat16), taps2, True)
    outputs = []
    for k in range(NT):
        tan_charge = deposit(tangents[k])
        t_one = mixing(point1, depth_ref(tan_charge, taps1, False).astype(jnp.bfloat16))
        moved = (dsilu(pre1) * t_one).astype(jnp.bfloat16)
        dz_two = mixing(point2, depth_ref(moved, taps2, False).astype(jnp.bfloat16))
        dg_two = (ddsilu(pre2) * scale * dz_two).astype(jnp.bfloat16)
        dg_one = depth_ref(mixing(point2.T, dg_two).astype(jnp.bfloat16), taps2, True)
        energy_term = (ddsilu(pre1) * t_one * g_one + dsilu(pre1) * dg_one).astype(jnp.bfloat16)
        back_one = mixing(point1.T, energy_term).astype(jnp.bfloat16)
        final = depth_ref(back_one, taps1, True).astype(jnp.bfloat16).reshape(CH, -1)
        outputs.append(jnp.take(final, flat, axis=1).astype(jnp.float32) * tab)
    return jnp.stack(outputs)
```

```python
import functools

import jax
import jax.numpy as jnp
from jax import lax
from jax.experimental import pallas as pl
from jax.experimental.pallas import tpu as pltpu
from jax.sharding import PartitionSpec as P

NG = 64
CH = 64
NT = 4
KSETS = 8
LANES = 2 * CH
HALF = NG // 2
GROUP = 4
VMEM_LIMIT = 56 * 1024 * 1024
F32 = jnp.float32
BF16 = jnp.bfloat16


def params():
    return pltpu.CompilerParams(vmem_limit_bytes=VMEM_LIMIT)


def cost(flops, nbytes):
    return pl.CostEstimate(flops=flops, bytes_accessed=nbytes, transcendentals=0)


def vmem():
    return pl.BlockSpec(memory_space=pltpu.VMEM)


def smem():
    return pl.BlockSpec(memory_space=pltpu.SMEM)


def deposits_kernel(peers, me_ref, feat_ref, tan_ref, sten_ref, table_ref, tab_ref, *outs):
    me = me_ref[0]
    count = feat_ref.shape[1]
    step = min(256, count)
    columns = [table_ref[:, s : s + 1] for s in range(KSETS)]
    for start in range(0, count, step):
        at = pl.ds(start, step)
        kinds = jnp.broadcast_to(sten_ref[:, at], (CH, step))
        tab = jnp.zeros((CH, step), F32)
        for s in range(KSETS):
            tab = jnp.where(kinds == s, columns[s], tab)
        tab_ref[:, at] = tab
        first = (feat_ref[:, at].astype(F32) * tab).astype(BF16)
        for j in range(peers):
            outs[j][:CH, at] = first
            own = tan_ref[lax.rem(lax.bitwise_xor(me, j), NT), :, at]
            outs[j][CH:, at] = (own.astype(F32) * tab).astype(BF16)


def make_deposits(me, features, tangents, stencil, table, peers):
    count = features.shape[1]
    out_shape = [jax.ShapeDtypeStruct((CH, count), F32)]
    out_shape += [jax.ShapeDtypeStruct((LANES, count), BF16)] * peers
    return pl.pallas_call(
        functools.partial(deposits_kernel, peers),
        out_shape=out_shape,
        in_specs=[smem()] + [vmem()] * 4,
        out_specs=[vmem()] * (peers + 1),
        compiler_params=params(),
        name="deposits",
    )(me, features, tangents, stencil.reshape(1, count), table.T)


def charge_kernel(peers, depth, *refs):
    cells, chunks = refs[:peers], refs[peers : 2 * peers]
    q_ref, low_ref, high_ref, grid_ref, rows_ref = refs[2 * peers :]
    step = pl.program_id(0)
    count = rows_ref.shape[0]
    unroll = 8

    @pl.when(step == 0)
    def _():
        def clear(i, carry):
            grid_ref[pl.ds(pl.multiple_of(i * 256, 256), 256), :] = jnp.zeros((256, LANES), F32)
            return carry

        lax.fori_loop(0, grid_ref.shape[0] // 256, clear, 0)
        for j in range(peers):
            for start in range(0, count, 256):
                block = chunks[j][:, start : start + 256].astype(F32)
                rows_ref[start : start + 256, :] = block.T

            def add(i, carry, j=j):
                for t in range(unroll):
                    atom = i * unroll + t
                    cell = cells[j][atom]
                    grid_ref[pl.ds(cell, 1), :] += rows_ref[pl.ds(atom, 1), :]
                return carry

            lax.fori_loop(0, count // unroll, add, 0)

    @pl.when(step > 0)
    def _():
        layer = step - 1

        def finish(y, carry):
            at = pl.multiple_of((layer * NG + y) * NG, NG)
            q_ref[0, y] = grid_ref[pl.ds(at, NG), :].astype(BF16)
            return carry

        lax.fori_loop(0, NG, finish, 0)

        @pl.when(layer == 0)
        def _():
            low_ref[...] = q_ref[...]

        @pl.when(layer == depth - 1)
        def _():
            high_ref[...] = q_ref[...]


def make_charge(cells, chunks, depth):
    peers = len(chunks)
    count = chunks[0].shape[1]
    layer = (1, NG, NG, LANES)
    edge = pl.BlockSpec(layer, lambda s: (0, 0, 0, 0))
    return pl.pallas_call(
        functools.partial(charge_kernel, peers, depth),
        grid=(depth + 1,),
        out_shape=[
            jax.ShapeDtypeStruct((depth, NG, NG, LANES), BF16),
            jax.ShapeDtypeStruct(layer, BF16),
            jax.ShapeDtypeStruct(layer, BF16),
        ],
        in_specs=[smem()] * peers + [vmem()] * peers,
        out_specs=[
            pl.BlockSpec(layer, lambda s: (jnp.maximum(s - 1, 0), 0, 0, 0)),
            edge,
            edge,
        ],
        scratch_shapes=[
            pltpu.VMEM((depth * NG * NG, LANES), F32),
            pltpu.VMEM((count, LANES), F32),
        ],
        compiler_params=params(),
        name="charge",
    )(*cells, *chunks)


def spread(weights, value):
    rows = value.shape[0]
    return (value.reshape(rows // 8, 8, LANES) * weights[None]).reshape(rows, LANES)


def taps_of(w_ref, axis):
    return [w_ref[3 * axis + t] for t in range(3)]


def weigh(w, low, mid, high):
    return spread(w[0], low) + spread(w[1], mid) + spread(w[2], high)


def along_z(w, low, mid, high, u_ref, rows, offset):
    def body(y, carry):
        u_ref[y + offset] = weigh(
            w, low[0, y].astype(F32), mid[0, y].astype(F32), high[0, y].astype(F32)
        )
        return carry

    lax.fori_loop(0, rows, body, 0, unroll=2)


def wrap_halves(u_ref):
    u_ref[0] = pltpu.roll(u_ref[HALF], CH, 1)
    u_ref[HALF + 1] = pltpu.roll(u_ref[1], CH, 1)


def along_yx(wy, wx, u_ref, before, here, after):
    v = weigh(wy, u_ref[before], u_ref[here], u_ref[after])
    return weigh(wx, pltpu.roll(v, 1, 0), v, pltpu.roll(v, NG - 1, 0))


def sigmoid(v):
    return 1.0 / (1.0 + jnp.exp(-v))


def first_stage(refs, u_refs, outs):
    w_ref, mix_ref, bias_ref = refs
    (u_ref,) = u_refs
    h_ref, m_ref, a_ref, b_ref = outs
    wy, wx = taps_of(w_ref, 1), taps_of(w_ref, 2)

    def body(i, carry):
        rows = []
        for t in range(GROUP):
            y = i * GROUP + t
            top = along_yx(wy, wx, u_ref, jnp.bitwise_and(y + NG - 1, NG - 1), y, y + 1)
            z = y + HALF
            end = along_yx(wy, wx, u_ref, z - 1, z, jnp.bitwise_and(z + 1, NG - 1))
            rows.append(jnp.concatenate([top.astype(BF16), end.astype(BF16)], 1))
        mixed = jnp.dot(jnp.concatenate(rows, 0), mix_ref[...], preferred_element_type=F32)
        for t in range(GROUP):
            y = i * GROUP + t
            part = mixed[t * NG : (t + 1) * NG]
            pre = part[:, :LANES] + bias_ref[...]
            tangent = part[:, LANES:]
            sg = sigmoid(pre)
            rest = 1.0 - sg
            slope = sg * (1.0 + pre * rest)
            curve = sg * rest * (2.0 + pre * (1.0 - 2.0 * sg))
            h_ref[0, y] = (pre * sg).astype(BF16)
            m_ref[0, y] = (slope * tangent).astype(BF16)
            a_ref[0, y] = curve * tangent
            b_ref[0, y] = slope
        return carry

    lax.fori_loop(0, HALF // GROUP, body, 0)


def second_stage(refs, u_refs, outs):
    w_ref, mix_ref, back_ref, bias_ref, scale_ref = refs
    uh_ref, um_ref = u_refs
    rh_ref, rm_ref = outs
    wy, wx = taps_of(w_ref, 1), taps_of(w_ref, 2)

    def body(i, carry):
        rows = []
        for t in range(GROUP):
            y = i * GROUP + t
            sh = along_yx(wy, wx, uh_ref, y, y + 1, y + 2)
            sm = along_yx(wy, wx, um_ref, y, y + 1, y + 2)
            rows.append(jnp.concatenate([sh.astype(BF16), sm.astype(BF16)], 1))
        mixed = jnp.dot(jnp.concatenate(rows, 0), mix_ref[...], preferred_element_type=F32)
        pre = mixed[:, :LANES] + bias_ref[...]
        sg = sigmoid(pre)
        rest = 1.0 - sg
        scale = scale_ref[...]
        grad = sg * (1.0 + pre * rest) * scale
        bend = sg * rest * (2.0 + pre * (1.0 - 2.0 * sg)) * scale * mixed[:, LANES:]
        both = jnp.concatenate([grad.astype(BF16), bend.astype(BF16)], 1)
        back = jnp.dot(both, back_ref[...], preferred_element_type=F32).astype(BF16)
        for t in range(GROUP):
            y = i * GROUP + t
            rh_ref[0, y] = back[t * NG : (t + 1) * NG, :LANES]
            rm_ref[0, y] = back[t * NG : (t + 1) * NG, LANES:]
        return carry

    lax.fori_loop(0, HALF // GROUP, body, 0)


def third_stage(refs, u_refs, outs):
    w_ref, back_ref, a_ref, b_ref = refs
    uh_ref, um_ref = u_refs
    (y_ref,) = outs
    wy, wx = taps_of(w_ref, 1), taps_of(w_ref, 2)

    def body(i, carry):
        rows = []
        for t in range(GROUP):
            y = i * GROUP + t
            g = along_yx(wy, wx, uh_ref, y, y + 1, y + 2)
            dg = along_yx(wy, wx, um_ref, y, y + 1, y + 2)
            rows.append((a_ref[0, y] * g + b_ref[0, y] * dg).astype(BF16))
        back = jnp.dot(jnp.concatenate(rows, 0), back_ref[...], preferred_element_type=F32)
        for t in range(GROUP):
            y_ref[0, i * GROUP + t] = back[t * NG : (t + 1) * NG].astype(BF16)
        return carry

    lax.fori_loop(0, HALF // GROUP, body, 0)


def fourth_stage(refs, u_refs, outs):
    (w_ref,) = refs
    (u_ref,) = u_refs
    (f_ref,) = outs
    wy, wx = taps_of(w_ref, 1), taps_of(w_ref, 2)

    def body(i, carry):
        for t in range(2):
            y = i * 2 + t
            f_ref[0, y] = along_yx(wy, wx, u_ref, y, y + 1, y + 2).astype(BF16).astype(F32)
        return carry

    lax.fori_loop(0, HALF // 2, body, 0)


STAGES = {
    "first": (first_stage, NG, (BF16, BF16, F32, F32), (0, 1)),
    "second": (second_stage, HALF, (BF16, BF16), (0, 1)),
    "third": (third_stage, HALF, (BF16,), (0,)),
    "fourth": (fourth_stage, HALF, (F32,), ()),
}


def stage_kernel(stage, edges, n_field, n_const, n_local, refs):
    body, rows, kinds, sent = STAGES[stage]
    refs = list(refs)

    def take(n):
        got = refs[:n]
        del refs[:n]
        return got

    consts = take(n_const)
    fields = [take(4 if edges else 3) for _ in range(n_field)]
    local = take(n_local)
    if edges:
        take(len(kinds))
    outs = take(len(kinds))
    sends = [take(2) for _ in sent] if edges else []
    u_refs = refs
    offset = 0 if rows == NG else 1
    wz = taps_of(consts[0], 0)
    for field, u_ref in zip(fields, u_refs):
        if edges:
            step = pl.program_id(0)
            below, here, inner, above = field

            @pl.when(step == 0)
            def _():
                along_z(wz, below, here, inner, u_ref, rows, offset)

            @pl.when(step == 1)
            def _():
                along_z(wz, inner, here, above, u_ref, rows, offset)
        else:
            along_z(wz, *field, u_ref, rows, offset)
        if offset:
            wrap_halves(u_ref)
    body(consts + local, u_refs, outs)
    for index, (low_ref, high_ref) in zip(sent, sends):

        @pl.when(step == 0)
        def _():
            low_ref[...] = outs[index][...]

        @pl.when(step == 1)
        def _():
            high_ref[...] = outs[index][...]


def run_stage(stage, depth, consts, fields, local, edge_halos=None, previous=None):
    body, rows, kinds, sent = STAGES[stage]
    edges = edge_halos is not None
    last = depth - 1
    in_layer = (1, rows, NG, LANES)
    out_layer = (1, HALF, NG, LANES)

    def whole(array):
        nil = (0,) * array.ndim
        return pl.BlockSpec(array.shape, lambda s: nil)

    def layer(shape, where):
        return pl.BlockSpec(shape, lambda s: (where(s), 0, 0, 0))

    def fixed(shape):
        return pl.BlockSpec(shape, lambda s: (0, 0, 0, 0))

    args, specs = list(consts), [whole(c) for c in consts]
    if edges:
        at = lambda s: s * last
        for field, (below, above) in zip(fields, edge_halos):
            args += [below, field, field, above]
            specs += [
                fixed(in_layer),
                layer(in_layer, at),
                layer(in_layer, lambda s: 1 + s * (last - 2)),
                fixed(in_layer),
            ]
        steps = 2
    else:
        at = lambda s: s + 1
        for field in fields:
            args += [field, field, field]
            specs += [
                layer(in_layer, lambda s: s),
                layer(in_layer, lambda s: s + 1),
                layer(in_layer, lambda s: s + 2),
            ]
        steps = depth - 2
    for array in local:
        args.append(array)
        specs.append(layer(out_layer, at))
    aliases = {}
    if edges:
        for i, array in enumerate(previous):
            aliases[len(args)] = i
            args.append(array)
            specs.append(pl.BlockSpec(memory_space=pl.ANY))
    out_shape = [jax.ShapeDtypeStruct((depth, HALF, NG, LANES), k) for k in kinds]
    out_specs = [layer(out_layer, at) for _ in kinds]
    if edges:
        for index in sent:
            out_shape += [jax.ShapeDtypeStruct(out_layer, kinds[index])] * 2
            out_specs += [fixed(out_layer)] * 2
    u_rows = NG if rows == NG else HALF + 2
    outs = pl.pallas_call(
        lambda *refs: stage_kernel(stage, edges, len(fields), len(consts), len(local), refs),
        grid=(steps,),
        out_shape=out_shape,
        in_specs=specs,
        out_specs=out_specs,
        scratch_shapes=[pltpu.VMEM((u_rows, NG, LANES), F32) for _ in fields],
        input_output_aliases=aliases,
        compiler_params=params(),
        cost_estimate=cost(steps * 4_000_000_000, steps * 6_000_000),
        name=stage + ("_edges" if edges else "_inner"),
    )(*args)
    full = list(outs[: len(kinds)])
    if not edges:
        return full
    sends = outs[len(kinds) :]
    return full, [(sends[2 * i], sends[2 * i + 1]) for i in range(len(sent))]


def exchange(pairs):
    size = lax.axis_size("slab")
    up = [(i, (i + 1) % size) for i in range(size)]
    down = [(j, i) for i, j in up]
    return [
        (lax.ppermute(high, "slab", up), lax.ppermute(low, "slab", down)) for low, high in pairs
    ]


def gather_kernel(peers, *refs):
    spots, halves = refs[:peers], refs[peers : 2 * peers]
    f_ref = refs[2 * peers]
    outs = refs[2 * peers + 1 : 3 * peers + 1]
    rows_ref = refs[-1]
    count = rows_ref.shape[0]
    unroll = 16
    eye = jnp.where(
        lax.broadcasted_iota(jnp.int32, (LANES, LANES), 0)
        == lax.broadcasted_iota(jnp.int32, (LANES, LANES), 1),
        1.0,
        0.0,
    ).astype(BF16)
    for j in range(peers):

        def pick(i, carry, j=j):
            for t in range(unroll):
                atom = i * unroll + t
                rows_ref[pl.ds(atom, 1), :] = f_ref[pl.ds(spots[j][atom], 1), :]
            return carry

        lax.fori_loop(0, count // unroll, pick, 0)
        for start in range(0, count, 256):
            block = rows_ref[start : start + 256, :].astype(BF16)
            turned = lax.dot_general(
                eye, block, (((1,), (1,)), ((), ())), preferred_element_type=F32
            )
            later = jnp.broadcast_to(halves[j][:, start : start + 256], (CH, 256)) == 1
            outs[j][:, start : start + 256] = jnp.where(later, turned[CH:], turned[:CH]).astype(
                BF16
            )


def make_gather(spots, halves, field):
    peers = len(spots)
    count = spots[0].shape[0]
    return pl.pallas_call(
        functools.partial(gather_kernel, peers),
        out_shape=[jax.ShapeDtypeStruct((CH, count), BF16)] * peers,
        in_specs=[smem()] * peers + [vmem()] * (peers + 1),
        out_specs=[vmem()] * peers,
        scratch_shapes=[pltpu.VMEM((count, LANES), F32)],
        compiler_params=params(),
        name="gather",
    )(*spots, *[h.reshape(1, count) for h in halves], field)


def finish_kernel(peers, me_ref, tab_ref, *refs):
    out_ref = refs[peers]
    me = me_ref[0]
    for j in range(peers):
        k = lax.rem(lax.bitwise_xor(me, j), NT)
        out_ref[k] = refs[j][...].astype(F32) * tab_ref[...]


def make_output(me, tab, returned):
    return pl.pallas_call(
        functools.partial(finish_kernel, len(returned)),
        out_shape=jax.ShapeDtypeStruct((NT,) + tab.shape, F32),
        in_specs=[smem()] + [vmem()] * (len(returned) + 1),
        out_specs=vmem(),
        compiler_params=params(),
        name="finish",
    )(me, tab, *returned)


def swap(array, j):
    if j == 0:
        return array
    size = lax.axis_size("brick")
    return lax.ppermute(array, "brick", [(i, i ^ j) for i in range(size)])


def lane_taps(taps, flip):
    kernel = taps[:, ::-1, :] if flip else taps
    tiled = jnp.concatenate([kernel, kernel], -1).reshape(9, 1, LANES)
    return jnp.broadcast_to(tiled, (9, 8, LANES))


def twice(vector):
    return jnp.concatenate([vector, vector]).reshape(1, LANES)


def shards(
    features,
    tangents,
    route,
    cell_local,
    stencil,
    stencil_table,
    taps1,
    taps2,
    point1,
    point2,
    bias1,
    bias2,
    readout,
):
    bricks = lax.axis_size("brick")
    depth = NG // lax.axis_size("slab")
    width = NG // bricks
    me = lax.axis_index("brick").astype(jnp.int32)
    mine = me.reshape(1)

    z_part = cell_local // (width * NG)
    y_part = route[:, 0] * width + (cell_local // NG) % width
    x_part = cell_local % NG
    cell = (z_part * NG + y_part) * NG + x_part
    cells = [swap(cell, j) for j in range(bricks)]

    tab, *blocks = make_deposits(mine, features, tangents, stencil, stencil_table, bricks)
    chunks = [swap(block, j) for j, block in enumerate(blocks)]
    charge, q_low, q_high = make_charge(cells, chunks, depth)

    zero = jnp.zeros((CH, CH), BF16)
    p1t, p2t = point1.T, point2.T
    mix1 = jnp.block(
        [
            [p1t, zero, zero, zero],
            [zero, zero, p1t, zero],
            [zero, p1t, zero, zero],
            [zero, zero, zero, p1t],
        ]
    )
    eye4 = jnp.eye(4, dtype=BF16)
    mix2 = jnp.kron(eye4, p2t)
    back2 = jnp.kron(eye4, point2)
    back1 = jnp.kron(eye4[:2, :2], point1)
    w1, w2 = lane_taps(taps1, False), lane_taps(taps2, False)
    w1t, w2t = lane_taps(taps1, True), lane_taps(taps2, True)

    def both(stage, consts, fields, local, edges):
        halos = exchange(edges)
        inner = run_stage(stage, depth, consts, fields, local)
        return run_stage(stage, depth, consts, fields, local, halos, inner)

    consts = [w1, mix1, twice(bias1)]
    (h, m, bend, slope), sends = both("first", consts, [charge], [], [(q_low, q_high)])
    consts = [w2, mix2, back2, twice(bias2), twice(readout)]
    (rh, rm), sends = both("second", consts, [h, m], [], sends)
    (y,), sends = both("third", [w2t, back1], [rh, rm], [bend, slope], sends)
    (field,), _ = both("fourth", [w1t], [y], [], sends)

    y_of = [(c // NG) % NG for c in cells[:NT]]
    spots = [
        ((c // (NG * NG)) * HALF + yy % HALF) * NG + c % NG for c, yy in zip(cells[:NT], y_of)
    ]
    halves = [yy // HALF for yy in y_of]
    picked = make_gather(spots, halves, field.reshape(-1, LANES))
    returned = [swap(block, j) for j, block in enumerate(picked)]
    return make_output(mine, tab, returned)


def solution(mesh):
    placed = (
        P(None, ("slab", "brick")),
        P(None, None, ("slab", "brick")),
        P(("slab", "brick"), None),
        P(("slab", "brick")),
        P(("slab", "brick")),
        P(),
        P(),
        P(),
        P(),
        P(),
        P(),
        P(),
        P(),
    )
    return jax.shard_map(
        shards,
        mesh=mesh,
        in_specs=placed,
        out_specs=P(None, None, ("slab", "brick")),
        check_vma=False,
    )
```

```python
import functools

import jax
import jax.numpy as jnp
from jax import lax
from jax.experimental import pallas as pl
from jax.experimental.pallas import tpu as pltpu
from jax.sharding import PartitionSpec as P

NG = 64
CH = 64
NT = 4
KSETS = 8
LANES = 2 * CH
HALF = NG // 2
GROUP = 4
RUN = 8
BLOCK = 256
MIB = 1024 * 1024
F32 = jnp.float32
BF16 = jnp.bfloat16


def params(mib):
    return pltpu.CompilerParams(vmem_limit_bytes=mib * MIB)


def cost(flops, nbytes):
    return pl.CostEstimate(flops=flops, bytes_accessed=nbytes, transcendentals=0)


def vmem():
    return pl.BlockSpec(memory_space=pltpu.VMEM)


def smem():
    return pl.BlockSpec(memory_space=pltpu.SMEM)


def deposits_kernel(peers, me_ref, feat_ref, tan_ref, sten_ref, table_ref, tab_ref, *outs):
    me = me_ref[0]
    count = feat_ref.shape[1]
    step = min(256, count)
    table = table_ref[...].T
    columns = [table[:, s : s + 1] for s in range(KSETS)]
    for start in range(0, count, step):
        at = pl.ds(start, step)
        kinds = jnp.broadcast_to(sten_ref[:, at], (CH, step))
        tab = jnp.zeros((CH, step), F32)
        for s in range(KSETS):
            tab = jnp.where(kinds == s, columns[s], tab)
        tab_ref[:, at] = tab
        first = (feat_ref[:, at].astype(F32) * tab).astype(BF16)
        for j in range(peers):
            outs[j][:CH, at] = first
            own = tan_ref[lax.rem(lax.bitwise_xor(me, j), NT), :, at]
            outs[j][CH:, at] = (own.astype(F32) * tab).astype(BF16)


def make_deposits(me, features, tangents, stencil, table, peers):
    count = features.shape[1]
    out_shape = [jax.ShapeDtypeStruct((CH, count), F32)]
    out_shape += [jax.ShapeDtypeStruct((LANES, count), BF16)] * peers
    return pl.pallas_call(
        functools.partial(deposits_kernel, peers),
        out_shape=out_shape,
        in_specs=[smem()] + [vmem()] * 4,
        out_specs=[vmem()] * (peers + 1),
        compiler_params=params(8),
        name="deposits",
    )(me, features, tangents, stencil.reshape(1, count), table)


def charge_kernel(peers, *refs):
    cells, chunks = refs[:peers], refs[peers : 2 * peers]
    marks = refs[2 * peers : 3 * peers]
    low_ref, mid_ref, high_ref, one_ref, two_ref, rows_ref, early_ref = refs[3 * peers :]
    count = rows_ref.shape[0]
    width = early_ref.shape[0]
    middle = count // 2

    def clear(i, carry):
        at = pl.ds(pl.multiple_of(i * 256, 256), 256)
        one_ref[at, :] = jnp.zeros((256, LANES), F32)
        two_ref[at, :] = jnp.zeros((256, LANES), F32)
        return carry

    lax.fori_loop(0, one_ref.shape[0] // 256, clear, 0)
    row = lax.broadcasted_iota(jnp.int32, (width, width), 0)
    column = lax.broadcasted_iota(jnp.int32, (width, width), 1)
    early = (column <= row) & (row // RUN == column // RUN)
    early_ref[...] = jnp.where(early, 1.0, 0.0)
    for j in range(peers):

        def turn(i, carry, j=j):
            at = pl.ds(pl.multiple_of(i * width, width), width)
            here = jnp.broadcast_to(marks[j][:, at].astype(F32), (width, width))
            taken = jnp.where(here.T == here, early_ref[...], 0.0).astype(BF16)
            rows_ref[at, :] = lax.dot_general(
                taken, chunks[j][:, at], (((1,), (1,)), ((), ())), preferred_element_type=F32
            )
            return carry

        lax.fori_loop(0, count // width, turn, 0)

        def add(i, carry, j=j):
            for group in range(2):
                at = (i * 2 + group) * RUN
                firsts = ((one_ref, at), (two_ref, middle + at))
                where = [[cells[j][first + t] for t in range(RUN)] for _, first in firsts]
                sums = [
                    [
                        ref[pl.ds(cell, 1), :] + rows_ref[pl.ds(first + t, 1), :]
                        for t, cell in enumerate(spots)
                    ]
                    for (ref, first), spots in zip(firsts, where)
                ]
                for (ref, _), spots, values in zip(firsts, where, sums):
                    for cell, value in zip(spots, values):
                        ref[pl.ds(cell, 1), :] = value
            return carry

        lax.fori_loop(0, middle // (2 * RUN), add, 0)

    def finish(base, out_ref, index):
        def body(y, carry):
            at = pl.ds(pl.multiple_of(base + y * NG, NG), NG)
            out_ref[index, y] = (one_ref[at, :] + two_ref[at, :]).astype(BF16)
            return carry

        lax.fori_loop(0, NG, body, 0, unroll=4)

    inner = mid_ref.shape[0]
    finish(0, low_ref, 0)
    finish((inner + 1) * NG * NG, high_ref, 0)

    def between(z, carry):
        finish((z + 1) * NG * NG, mid_ref, z)
        return carry

    lax.fori_loop(0, inner, between, 0)


def make_charge(cells, chunks, depth):
    peers = len(chunks)
    count = chunks[0].shape[1]
    width = min(BLOCK, count)
    layers = [
        jax.ShapeDtypeStruct((n, NG, NG, LANES), BF16) for n in (1, depth - 2, 1)
    ]
    slab = pltpu.VMEM((depth * NG * NG, LANES), F32)
    return pl.pallas_call(
        functools.partial(charge_kernel, peers),
        out_shape=layers,
        in_specs=[smem()] * peers + [vmem()] * (2 * peers),
        out_specs=[vmem()] * 3,
        scratch_shapes=[
            slab,
            slab,
            pltpu.VMEM((count, LANES), F32),
            pltpu.VMEM((width, width), F32),
        ],
        compiler_params=params(40),
        name="charge",
    )(*cells, *chunks, *[c.reshape(1, count) for c in cells])


ROW_BIAS1, ROW_BIAS2, ROW_SCALE, ROW_HALF = 18, 19, 20, 21


def weights_kernel(p1_ref, p2_ref, t1_ref, t2_ref, b1_ref, b2_ref, r_ref, *outs):
    mix1_ref, mix2_ref, back2_ref, back1_ref, lanes_ref = outs
    p1, p2 = p1_ref[...].astype(F32), p2_ref[...].astype(F32)
    p1t, p2t = 0.5 * p1.T, 0.5 * p2.T
    zero = jnp.zeros((CH, CH), F32)

    def fill(ref, block, order):
        for i, place in enumerate(order):
            parts = [block if j == place else zero for j in range(len(order))]
            ref[i * CH : (i + 1) * CH, :] = jnp.concatenate(parts, 1).astype(BF16)

    fill(mix1_ref, p1t, (0, 2, 1, 3))
    fill(mix2_ref, p2t, (0, 1, 2, 3))
    fill(back2_ref, p2, (0, 1, 2, 3))
    fill(back1_ref, p1, (0, 1))

    def put(row, value):
        lanes_ref[row : row + 1, :] = jnp.concatenate([value, value], 1)

    for axis in range(3):
        for t in range(3):
            put(3 * axis + t, t1_ref[axis, t : t + 1, :])
            put(9 + 3 * axis + t, t2_ref[axis, t : t + 1, :])
    for t in range(3):
        put(ROW_HALF + t, 0.5 * t2_ref[2, t : t + 1, :])
    put(ROW_BIAS1, 0.5 * b1_ref[...])
    put(ROW_BIAS2, 0.5 * b2_ref[...])
    put(ROW_SCALE, r_ref[...])


def make_weights(point1, point2, taps1, taps2, bias1, bias2, readout):
    wide = jax.ShapeDtypeStruct((2 * LANES, 2 * LANES), BF16)
    return pl.pallas_call(
        weights_kernel,
        out_shape=[
            wide,
            wide,
            wide,
            jax.ShapeDtypeStruct((LANES, LANES), BF16),
            jax.ShapeDtypeStruct((24, LANES), F32),
        ],
        in_specs=[vmem()] * 7,
        out_specs=[vmem()] * 5,
        compiler_params=params(4),
        name="weights",
    )(point1, point2, taps1, taps2, *[v.reshape(1, CH) for v in (bias1, bias2, readout)])


def spread(weights, value):
    rows = value.shape[0]
    return (value.reshape(rows // 8, 8, LANES) * weights[None]).reshape(rows, LANES)


def lane_row(w_ref, row):
    return jnp.broadcast_to(w_ref[row : row + 1, :], (8, LANES))


def taps_of(w_ref, start, flip):
    order = (2, 1, 0) if flip else (0, 1, 2)
    return [lane_row(w_ref, start + t) for t in order]


def weigh(w, low, mid, high):
    return spread(w[0], low) + spread(w[1], mid) + spread(w[2], high)


def along_z(w, around, u_ref, rows, offset):
    def body(y, carry):
        low, mid, high = (ref[index, y].astype(F32) for ref, index in around)
        u_ref[y + offset] = weigh(w, low, mid, high)
        return carry

    lax.fori_loop(0, rows, body, 0, unroll=2)


def keep_layer(new, slot, ring_ref, rows):
    ref, index = new

    def body(y, carry):
        ring_ref[slot, y] = ref[index, y].astype(F32)
        return carry

    lax.fori_loop(0, rows, body, 0, unroll=2)


def along_z_ring(w, new, step, ring_ref, u_ref, rows, offset):
    ref, index = new
    low, mid, high = (lax.rem(jnp.int32(step + t), jnp.int32(3)) for t in (1, 2, 0))

    def body(y, carry):
        last = ref[index, y].astype(F32)
        ring_ref[high, y] = last
        u_ref[y + offset] = weigh(w, ring_ref[low, y], ring_ref[mid, y], last)
        return carry

    lax.fori_loop(0, rows, body, 0, unroll=2)


def wrap_halves(u_ref):
    u_ref[0] = pltpu.roll(u_ref[HALF], CH, 1)
    u_ref[HALF + 1] = pltpu.roll(u_ref[1], CH, 1)


def along_y(wy, u_ref, before, here, after):
    return weigh(wy, u_ref[before], u_ref[here], u_ref[after])


def along_x(wx, value, v_ref, slot):
    v_ref[slot, 8 : 8 + NG] = value
    v_ref[slot, 7:8] = value[NG - 1 :]
    v_ref[slot, 8 + NG : 9 + NG] = value[:1]
    return weigh(wx, v_ref[slot, 7 : 7 + NG], value, v_ref[slot, 9 : 9 + NG])


def silu_terms(half):
    t = jnp.tanh(half)
    product = half * t
    bump = 1.0 - t * t
    return half + product, (1.0 + t) + half * bump, bump * (1.0 - product)


def first_stage(refs, u_refs, v_ref, outs, at):
    w_ref, mix_ref = refs
    (u_ref,) = u_refs
    h_ref, m_ref, a_ref, b_ref = outs
    wy, wx = taps_of(w_ref, 3, False), taps_of(w_ref, 6, False)
    bias = w_ref[ROW_BIAS1 : ROW_BIAS1 + 1, :]

    def body(i, carry):
        rows = []
        for t in range(GROUP):
            y = i * GROUP + t
            z = y + HALF
            top = along_y(wy, u_ref, jnp.bitwise_and(y + NG - 1, NG - 1), y, y + 1)
            end = along_y(wy, u_ref, z - 1, z, jnp.bitwise_and(z + 1, NG - 1))
            top = along_x(wx, top, v_ref, 2 * t).astype(BF16)
            end = along_x(wx, end, v_ref, 2 * t + 1).astype(BF16)
            rows.append(jnp.concatenate([top, end], 1))
        mixed = jnp.dot(jnp.concatenate(rows, 0), mix_ref[...], preferred_element_type=F32)
        for t in range(GROUP):
            y = i * GROUP + t
            part = mixed[t * NG : (t + 1) * NG]
            tangent = part[:, LANES:]
            value, slope, curve = silu_terms(part[:, :LANES] + bias)
            h_ref[at, y] = value.astype(BF16)
            m_ref[at, y] = (slope * tangent).astype(BF16)
            a_ref[at, y] = (curve * tangent).astype(a_ref.dtype)
            b_ref[at, y] = slope.astype(b_ref.dtype)
        return carry

    lax.fori_loop(0, HALF // GROUP, body, 0)


def second_stage(refs, u_refs, v_ref, outs, at):
    w_ref, mix_ref, back_ref = refs
    uh_ref, um_ref = u_refs
    rh_ref, rm_ref = outs
    wy, wx = taps_of(w_ref, 12, False), taps_of(w_ref, 15, False)
    bias = w_ref[ROW_BIAS2 : ROW_BIAS2 + 1, :]
    scale = w_ref[ROW_SCALE : ROW_SCALE + 1, :]

    def body(i, carry):
        rows = []
        for t in range(GROUP):
            y = i * GROUP + t
            sh = along_x(wx, along_y(wy, uh_ref, y, y + 1, y + 2), v_ref, 2 * t).astype(BF16)
            sm = along_x(wx, along_y(wy, um_ref, y, y + 1, y + 2), v_ref, 2 * t + 1).astype(BF16)
            rows.append(jnp.concatenate([sh, sm], 1))
        mixed = jnp.dot(jnp.concatenate(rows, 0), mix_ref[...], preferred_element_type=F32)
        _, slope, curve = silu_terms(mixed[:, :LANES] + bias)
        grad = slope * (0.5 * scale)
        bend = curve * scale * mixed[:, LANES:]
        both = jnp.concatenate([grad.astype(BF16), bend.astype(BF16)], 1)
        back = jnp.dot(both, back_ref[...], preferred_element_type=F32).astype(BF16)
        for t in range(GROUP):
            y = i * GROUP + t
            rh_ref[at, y] = back[t * NG : (t + 1) * NG, :LANES]
            rm_ref[at, y] = back[t * NG : (t + 1) * NG, LANES:]
        return carry

    lax.fori_loop(0, HALF // GROUP, body, 0)


def third_stage(refs, u_refs, v_ref, outs, at):
    w_ref, back_ref, a_ref, b_ref = refs
    uh_ref, um_ref = u_refs
    (y_ref,) = outs
    wy, wx = taps_of(w_ref, 12, True), taps_of(w_ref, 15, True)
    wx_half = taps_of(w_ref, ROW_HALF, True)

    def body(i, carry):
        rows = []
        for t in range(GROUP):
            y = i * GROUP + t
            g = along_x(wx, along_y(wy, uh_ref, y, y + 1, y + 2), v_ref, 2 * t)
            dg = along_x(wx_half, along_y(wy, um_ref, y, y + 1, y + 2), v_ref, 2 * t + 1)
            term = a_ref[at, y].astype(F32) * g + b_ref[at, y].astype(F32) * dg
            rows.append(term.astype(BF16))
        back = jnp.dot(jnp.concatenate(rows, 0), back_ref[...], preferred_element_type=F32)
        for t in range(GROUP):
            y_ref[at, i * GROUP + t] = back[t * NG : (t + 1) * NG].astype(BF16)
        return carry

    lax.fori_loop(0, HALF // GROUP, body, 0)


def fourth_rows(w_ref, u_ref, v_ref, put):
    wy, wx = taps_of(w_ref, 3, True), taps_of(w_ref, 6, True)

    def body(i, carry):
        for t in range(GROUP):
            y = i * GROUP + t
            out = along_x(wx, along_y(wy, u_ref, y, y + 1, y + 2), v_ref, t)
            put(y, out.astype(BF16).astype(F32))
        return carry

    lax.fori_loop(0, HALF // GROUP, body, 0)


def fourth_stage(refs, u_refs, v_ref, outs, at):
    def put(y, row):
        outs[0][at, y] = row

    fourth_rows(refs[0], u_refs[0], v_ref, put)


STAGES = {
    "first": (first_stage, NG, (BF16, BF16, F32, F32), (0, 1), (0, False)),
    "second": (second_stage, HALF, (BF16, BF16), (0, 1), (9, False)),
    "third": (third_stage, HALF, (BF16,), (0,), (9, True)),
    "fourth": (fourth_stage, HALF, (F32,), (), (0, True)),
}


def taker(refs):
    left = list(refs)

    def take(n):
        got = left[:n]
        del left[:n]
        return got

    return take


def inner_kernel(stage, n_const, n_field, n_local, *refs):
    body, rows, kinds, _, (start, flip) = STAGES[stage]
    take = taker(refs)
    consts = take(n_const)
    fields = [take(3) for _ in range(n_field)]
    local, outs = take(n_local), take(len(kinds))
    u_refs, ring_refs = take(n_field), take(n_field)
    (v_ref,) = take(1)
    offset = 0 if rows == NG else 1
    wz = taps_of(consts[0], start, flip)
    inner = fields[0][1].shape[0]

    def layer(step, which, index):
        for field, u_ref, ring_ref in zip(fields, u_refs, ring_refs):
            along_z_ring(wz, (field[which], index), step, ring_ref, u_ref, rows, offset)
            if offset:
                wrap_halves(u_ref)
        body(consts + local, u_refs, v_ref, outs, step - 2)

    def loop(step, carry):
        layer(step, 1, step - 1)
        return carry

    for (low_ref, mid_ref, _), ring_ref in zip(fields, ring_refs):
        keep_layer((low_ref, 0), 0, ring_ref, rows)
        keep_layer((mid_ref, 0), 1, ring_ref, rows)
    lax.fori_loop(2, inner + 1, loop, 0)
    layer(inner + 1, 2, 0)


def edge_kernel(stage, n_const, n_field, n_local, places, *refs):
    body, rows, kinds, _, (start, flip) = STAGES[stage]
    take = taker(refs)
    consts = take(n_const)
    fields = [take(3) for _ in range(n_field)]
    local, outs, u_refs = take(n_local), take(len(kinds)), take(n_field)
    (v_ref,) = take(1)
    offset = 0 if rows == NG else 1
    wz = taps_of(consts[0], start, flip)
    for field, u_ref in zip(fields, u_refs):
        along_z(wz, list(zip(field, places)), u_ref, rows, offset)
        if offset:
            wrap_halves(u_ref)
    body(consts + local, u_refs, v_ref, outs, 0)


def field_scratch(stage, n_field, ring):
    rows = STAGES[stage][1]
    u_rows = NG if rows == NG else HALF + 2
    scratch = [pltpu.VMEM((u_rows, NG, LANES), F32)] * n_field
    if ring:
        scratch += [pltpu.VMEM((3, rows, NG, LANES), F32)] * n_field
    return scratch + [pltpu.VMEM((2 * GROUP, NG + 16, LANES), F32)]


def call_stage(kernel, name, layers, mib, kinds, args, scratch):
    return pl.pallas_call(
        kernel,
        out_shape=[jax.ShapeDtypeStruct((layers, HALF, NG, LANES), k) for k in kinds],
        in_specs=[vmem()] * len(args),
        out_specs=[vmem()] * len(kinds),
        scratch_shapes=scratch,
        compiler_params=params(mib),
        cost_estimate=cost(layers * 4_000_000_000, layers * 6_000_000),
        name=name,
    )(*args)


def run_inner(stage, consts, fields, local):
    kernel = functools.partial(inner_kernel, stage, len(consts), len(fields), len(local))
    args = [*consts, *[ref for field in fields for ref in field], *[x[1] for x in local]]
    scratch = field_scratch(stage, len(fields), True)
    layers = fields[0][1].shape[0]
    return call_stage(kernel, stage + "_inner", layers, 16, STAGES[stage][2], args, scratch)


def run_edge(stage, consts, fields, local, halos, side):
    inner = fields[0][1].shape[0]
    around, places = [], (0, 0, 0) if side == 0 else (inner - 1, 0, 0)
    for (low, mid, high), (below, above) in zip(fields, halos):
        around += [below, low, mid] if side == 0 else [mid, high, above]
    kernel = functools.partial(
        edge_kernel, stage, len(consts), len(fields), len(local), places
    )
    args = [*consts, *around, *[x[2 * side] for x in local]]
    scratch = field_scratch(stage, len(fields), False)
    name = stage + ("_low", "_high")[side]
    return call_stage(kernel, name, 1, 8, STAGES[stage][2], args, scratch)


def exchange(fields):
    size = lax.axis_size("slab")
    up = [(i, (i + 1) % size) for i in range(size)]
    down = [(j, i) for i, j in up]
    return [
        (lax.ppermute(high, "slab", up), lax.ppermute(low, "slab", down))
        for low, _, high in fields
    ]


def gather_kernel(peers, depth, *refs):
    spots, halves = refs[:peers], refs[peers : 2 * peers]
    w_ref, below_ref, low_ref, mid_ref, high_ref, above_ref, inner_ref = refs[
        2 * peers : 2 * peers + 7
    ]
    outs = refs[2 * peers + 7 : 3 * peers + 7]
    f_ref, rows_ref, u_ref, v_ref, sem = refs[3 * peers + 7 :]
    count = rows_ref.shape[0]
    unroll = 16
    layer = HALF * NG
    fetch = pltpu.make_async_copy(inner_ref, f_ref.at[pl.ds(layer, (depth - 2) * layer)], sem)
    fetch.start()
    wz = taps_of(w_ref, 0, True)
    for base, around in (
        (0, ((below_ref, 0), (low_ref, 0), (mid_ref, 0))),
        ((depth - 1) * layer, ((mid_ref, depth - 3), (high_ref, 0), (above_ref, 0))),
    ):
        along_z(wz, around, u_ref, HALF, 1)
        wrap_halves(u_ref)

        def put(y, row, base=base):
            f_ref[pl.ds(pl.multiple_of(base + y * NG, NG), NG), :] = row

        fourth_rows(w_ref, u_ref, v_ref, put)
    fetch.wait()
    eye = jnp.where(
        lax.broadcasted_iota(jnp.int32, (LANES, LANES), 0)
        == lax.broadcasted_iota(jnp.int32, (LANES, LANES), 1),
        1.0,
        0.0,
    ).astype(BF16)
    width = min(256, count)
    for j in range(peers):

        def pick(i, carry, j=j):
            for t in range(unroll):
                atom = i * unroll + t
                rows_ref[pl.ds(atom, 1), :] = f_ref[pl.ds(spots[j][atom], 1), :]
            return carry

        lax.fori_loop(0, count // unroll, pick, 0)
        for start in range(0, count, width):
            at = slice(start, start + width)
            turned = lax.dot_general(
                eye,
                rows_ref[at, :].astype(BF16),
                (((1,), (1,)), ((), ())),
                preferred_element_type=F32,
            )
            later = jnp.broadcast_to(halves[j][:, at], (CH, width)) == 1
            outs[j][:, at] = jnp.where(later, turned[CH:], turned[:CH]).astype(BF16)


def make_gather(spots, halves, taps, y, halos, inner):
    peers = len(spots)
    count = spots[0].shape[0]
    low, mid, high = y
    below, above = halos
    depth = mid.shape[0] + 2
    return pl.pallas_call(
        functools.partial(gather_kernel, peers, depth),
        out_shape=[jax.ShapeDtypeStruct((CH, count), BF16)] * peers,
        in_specs=[smem()] * peers
        + [vmem()] * (peers + 6)
        + [pl.BlockSpec(memory_space=pl.ANY)],
        out_specs=[vmem()] * peers,
        scratch_shapes=[
            pltpu.VMEM((depth * HALF * NG, LANES), F32),
            pltpu.VMEM((count, LANES), F32),
            pltpu.VMEM((HALF + 2, NG, LANES), F32),
            pltpu.VMEM((2 * GROUP, NG + 16, LANES), F32),
            pltpu.SemaphoreType.DMA,
        ],
        compiler_params=params(16),
        name="gather",
    )(
        *spots,
        *[h.reshape(1, count) for h in halves],
        taps,
        below,
        low,
        mid,
        high,
        above,
        inner.reshape(-1, LANES),
    )


def finish_kernel(peers, me_ref, tab_ref, *refs):
    out_ref = refs[peers]
    me = me_ref[0]
    for j in range(peers):
        k = lax.rem(lax.bitwise_xor(me, j), NT)
        out_ref[k] = refs[j][...].astype(F32) * tab_ref[...]


def make_output(me, tab, returned):
    return pl.pallas_call(
        functools.partial(finish_kernel, len(returned)),
        out_shape=jax.ShapeDtypeStruct((NT,) + tab.shape, F32),
        in_specs=[smem()] + [vmem()] * (len(returned) + 1),
        out_specs=vmem(),
        compiler_params=params(8),
        name="finish",
    )(me, tab, *returned)


def swap(array, j):
    if j == 0:
        return array
    size = lax.axis_size("brick")
    return lax.ppermute(array, "brick", [(i, i ^ j) for i in range(size)])


def shards(
    features,
    tangents,
    route,
    cell_local,
    stencil,
    stencil_table,
    taps1,
    taps2,
    point1,
    point2,
    bias1,
    bias2,
    readout,
):
    bricks = lax.axis_size("brick")
    depth = NG // lax.axis_size("slab")
    width = NG // bricks
    me = lax.axis_index("brick").astype(jnp.int32)
    mine = me.reshape(1)

    tab, *blocks = make_deposits(mine, features, tangents, stencil, stencil_table, bricks)
    blocks, route, cell_local = lax.optimization_barrier((blocks, route, cell_local))
    chunks = [swap(block, j) for j, block in enumerate(blocks)]
    z_part = cell_local // (width * NG)
    y_part = route[:, 0] * width + (cell_local // NG) % width
    x_part = cell_local % NG
    cell = (z_part * NG + y_part) * NG + x_part
    cells = []
    for j in range(bricks):
        if j >= 3:
            cells[1], cell = lax.optimization_barrier((cells[1], cell))
        cells.append(swap(cell, j))
    charge = make_charge(cells, chunks, depth)

    mix1, mix2, back2, back1, lanes = make_weights(
        point1, point2, taps1, taps2, bias1, bias2, readout
    )

    def both(stage, consts, fields, local, halos):
        middle = run_inner(stage, consts, fields, local)
        lows = run_edge(stage, consts, fields, local, halos, 0)
        highs = run_edge(stage, consts, fields, local, halos, 1)
        return list(zip(lows, middle, highs))

    h, m, bend, slope = both("first", [lanes, mix1], [charge], [], exchange([charge]))
    rh, rm = both("second", [lanes, mix2, back2], [h, m], [], exchange([h, m]))
    (y,) = both("third", [lanes, back1], [rh, rm], [bend, slope], exchange([rh, rm]))
    ((below, above),) = exchange([y])
    (inner,) = run_inner("fourth", [lanes], [y], [])

    y_of = [(c // NG) % NG for c in cells[:NT]]
    spots = [
        ((c // (NG * NG)) * HALF + yy % HALF) * NG + c % NG for c, yy in zip(cells[:NT], y_of)
    ]
    halves = [yy // HALF for yy in y_of]
    picked = make_gather(spots, halves, lanes, y, (below, above), inner)
    returned = [swap(block, j) for j, block in enumerate(picked)]
    return make_output(mine, tab, returned)


def solution(mesh):
    placed = (
        P(None, ("slab", "brick")),
        P(None, None, ("slab", "brick")),
        P(("slab", "brick"), None),
        P(("slab", "brick")),
        P(("slab", "brick")),
        P(),
        P(),
        P(),
        P(),
        P(),
        P(),
        P(),
        P(),
    )
    return jax.shard_map(
        shards,
        mesh=mesh,
        in_specs=placed,
        out_specs=P(None, None, ("slab", "brick")),
        check_vma=False,
    )
```

```python
import functools

import jax
import jax.numpy as jnp
from jax import lax
from jax.experimental import pallas as pl
from jax.experimental.pallas import tpu as pltpu
from jax.sharding import PartitionSpec as P

NG = 64
CH = 64
NT = 4
KSETS = 8
LANES = 2 * CH
HALF = NG // 2
GROUP = 8
ROWS = 4
RUN = 16
BLOCK = 256
MIB = 1024 * 1024
F32 = jnp.float32
BF16 = jnp.bfloat16


def params(mib):
    return pltpu.CompilerParams(vmem_limit_bytes=mib * MIB)


def cost(flops, nbytes):
    return pl.CostEstimate(flops=flops, bytes_accessed=nbytes, transcendentals=0)


def vmem():
    return pl.BlockSpec(memory_space=pltpu.VMEM)


def smem():
    return pl.BlockSpec(memory_space=pltpu.SMEM)


def deposits_kernel(peers, me_ref, feat_ref, tan_ref, sten_ref, table_ref, tab_ref, *refs):
    outs = refs[:peers]
    feat, tan, sten, rows, sems, small = refs[peers:]
    me = me_ref[0]
    parts, _, step = feat.shape
    kinds_copy = pltpu.make_async_copy(sten_ref, sten, small.at[0])
    table_copy = pltpu.make_async_copy(table_ref, rows, small.at[1])
    kinds_copy.start()
    table_copy.start()
    copies = []
    for p in range(parts):
        at = pl.ds(p * step, step)
        pair = (
            pltpu.make_async_copy(feat_ref.at[:, at], feat.at[p], sems.at[p, 0]),
            pltpu.make_async_copy(tan_ref.at[:, :, at], tan.at[p], sems.at[p, 1]),
        )
        for copy in pair:
            copy.start()
        copies.append(pair)
    kinds_copy.wait()
    table_copy.wait()
    table = rows[...].T
    for p in range(parts):
        at = pl.ds(p * step, step)
        kinds = jnp.broadcast_to(sten[:, at], (CH, step))
        tab = jnp.zeros((CH, step), F32)
        for s in range(KSETS):
            tab = jnp.where(kinds == s, table[:, s : s + 1], tab)
        tab_ref[:, at] = tab
        for copy in copies[p]:
            copy.wait()
        first = (feat[p].astype(F32) * tab).astype(BF16)
        for j in range(peers):
            outs[j][:CH, at] = first
            own = tan[p, lax.rem(lax.bitwise_xor(me, j), NT)]
            outs[j][CH:, at] = (own.astype(F32) * tab).astype(BF16)


def make_deposits(me, features, tangents, stencil, table, peers):
    count = features.shape[1]
    step = min(512, count)
    parts = count // step
    far = pl.BlockSpec(memory_space=pltpu.HBM)
    out_shape = [jax.ShapeDtypeStruct((CH, count), F32)]
    out_shape += [jax.ShapeDtypeStruct((LANES, count), BF16)] * peers
    return pl.pallas_call(
        functools.partial(deposits_kernel, peers),
        out_shape=out_shape,
        in_specs=[smem()] + [far] * 4,
        out_specs=[vmem()] * (peers + 1),
        scratch_shapes=[
            pltpu.VMEM((parts, CH, step), BF16),
            pltpu.VMEM((parts, NT, CH, step), BF16),
            pltpu.VMEM((1, count), jnp.int32),
            pltpu.VMEM(table.shape, F32),
            pltpu.SemaphoreType.DMA((parts, 2)),
            pltpu.SemaphoreType.DMA((2,)),
        ],
        compiler_params=params(8),
        name="deposits",
    )(me, features, tangents, stencil.reshape(1, count), table)


def clear(ref):
    def body(i, carry):
        at = pl.ds(pl.multiple_of(i * 256, 256), 256)
        ref[at, :] = jnp.zeros((256, LANES), F32)
        return carry

    lax.fori_loop(0, ref.shape[0] // 256, body, 0)


def scatter(cells, chunks, marks, sums_ref, rows_ref, early_ref):
    width = early_ref.shape[0]
    blocks = rows_ref.shape[0] // width
    row = lax.broadcasted_iota(jnp.int32, (width, width), 0)
    column = lax.broadcasted_iota(jnp.int32, (width, width), 1)
    early = (column <= row) & (row // RUN == column // RUN)
    early_ref[...] = jnp.where(early, 1.0, 0.0)
    for cell_ref, chunk_ref, mark_ref in zip(cells, chunks, marks):

        def turn(i, carry):
            at = pl.ds(pl.multiple_of(i * width, width), width)
            here = jnp.broadcast_to(mark_ref[:, at].astype(F32), (width, width))
            taken = jnp.where(here.T == here, early_ref[...], 0.0).astype(BF16)
            rows_ref[at, :] = lax.dot_general(
                taken, chunk_ref[:, at], (((1,), (1,)), ((), ())), preferred_element_type=F32
            )
            return carry

        lax.fori_loop(0, blocks, turn, 0, unroll=2)

        def add(i, carry):
            first = i * RUN
            where = [cell_ref[first + t] for t in range(RUN)]
            sums = [
                sums_ref[pl.ds(cell, 1), :] + rows_ref[pl.ds(first + t, 1), :]
                for t, cell in enumerate(where)
            ]
            for cell, value in zip(where, sums):
                sums_ref[pl.ds(cell, 1), :] = value
            return carry

        lax.fori_loop(0, blocks * width // RUN, add, 0)


def split_scatter(peers, refs):
    cells, chunks = refs[:peers], refs[peers : 2 * peers]
    return cells, chunks, refs[2 * peers : 3 * peers], refs[3 * peers :]


def first_sums_kernel(peers, *refs):
    cells, chunks, marks, (sums_ref, rows_ref, early_ref) = split_scatter(peers, refs)
    clear(sums_ref)
    scatter(cells, chunks, marks, sums_ref, rows_ref, early_ref)


def more_sums_kernel(peers, *refs):
    cells, chunks, marks, (_, sums_ref, rows_ref, early_ref) = split_scatter(peers, refs)
    scatter(cells, chunks, marks, sums_ref, rows_ref, early_ref)


def charge_kernel(peers, *refs):
    cells, chunks, marks, rest = split_scatter(peers, refs)
    _, sums_ref, low_ref, mid_ref, high_ref, rows_ref, early_ref = rest
    scatter(cells, chunks, marks, sums_ref, rows_ref, early_ref)

    def finish(base, out_ref, index):
        def body(y, carry):
            at = pl.ds(pl.multiple_of(base + y * NG, NG), NG)
            out_ref[index, y] = sums_ref[at, :].astype(BF16)
            return carry

        lax.fori_loop(0, NG, body, 0, unroll=4)

    inner = mid_ref.shape[0]
    finish(0, low_ref, 0)
    finish((inner + 1) * NG * NG, high_ref, 0)

    def between(z, carry):
        finish((z + 1) * NG * NG, mid_ref, z)
        return carry

    lax.fori_loop(0, inner, between, 0)


def run_scatter(kernel, name, cells, chunks, sums, depth):
    peers, count = len(cells), cells[0].shape[0]
    width = min(BLOCK, count)
    args = [*cells, *chunks, *[c.reshape(1, count) for c in cells]]
    specs = [smem()] * peers + [vmem()] * (2 * peers)
    out_shape = [jax.ShapeDtypeStruct((depth * NG * NG, LANES), F32)]
    aliases = {}
    if sums is not None:
        aliases[len(args)] = 0
        args.append(sums)
        specs.append(vmem())
    if kernel is charge_kernel:
        out_shape += [jax.ShapeDtypeStruct((n, NG, NG, LANES), BF16) for n in (1, depth - 2, 1)]
    return pl.pallas_call(
        functools.partial(kernel, peers),
        out_shape=out_shape,
        in_specs=specs,
        out_specs=[vmem()] * len(out_shape),
        scratch_shapes=[pltpu.VMEM((count, LANES), F32), pltpu.VMEM((width, width), F32)],
        input_output_aliases=aliases,
        compiler_params=params(6),
        cost_estimate=cost(peers * 4_000_000_000, peers * 8_000_000),
        name=name,
    )(*args)


ROW_BIAS1, ROW_BIAS2, ROW_SCALE, ROW_HALF = 18, 19, 20, 21


def weights_kernel(p1_ref, p2_ref, t1_ref, t2_ref, b1_ref, b2_ref, r_ref, *outs):
    mix1_ref, mix2_ref, back2_ref, back1_ref, lanes_ref = outs
    p1, p2 = p1_ref[...].astype(F32), p2_ref[...].astype(F32)
    p1t, p2t = 0.5 * p1.T, 0.5 * p2.T
    zero = jnp.zeros((CH, CH), F32)

    def fill(ref, block, order):
        for i, place in enumerate(order):
            parts = [block if j == place else zero for j in range(len(order))]
            ref[i * CH : (i + 1) * CH, :] = jnp.concatenate(parts, 1).astype(BF16)

    fill(mix1_ref, p1t, (0, 2, 1, 3))
    fill(mix2_ref, p2t, (0, 1, 2, 3))
    fill(back2_ref, p2, (0, 1, 2, 3))
    fill(back1_ref, p1, (0, 1))

    def put(row, value):
        lanes_ref[row : row + 1, :] = jnp.concatenate([value, value], 1)

    for axis in range(3):
        for t in range(3):
            put(3 * axis + t, t1_ref[axis, t : t + 1, :])
            put(9 + 3 * axis + t, t2_ref[axis, t : t + 1, :])
    for t in range(3):
        put(ROW_HALF + t, 0.5 * t2_ref[2, t : t + 1, :])
    put(ROW_BIAS1, 0.5 * b1_ref[...])
    put(ROW_BIAS2, 0.5 * b2_ref[...])
    put(ROW_SCALE, r_ref[...])


def make_weights(point1, point2, taps1, taps2, bias1, bias2, readout):
    wide = jax.ShapeDtypeStruct((2 * LANES, 2 * LANES), BF16)
    return pl.pallas_call(
        weights_kernel,
        out_shape=[
            wide,
            wide,
            wide,
            jax.ShapeDtypeStruct((LANES, LANES), BF16),
            jax.ShapeDtypeStruct((24, LANES), F32),
        ],
        in_specs=[vmem()] * 7,
        out_specs=[vmem()] * 5,
        compiler_params=params(4),
        name="weights",
    )(point1, point2, taps1, taps2, *[v.reshape(1, CH) for v in (bias1, bias2, readout)])


def spread(weights, value):
    rows = value.shape[0]
    return (value.reshape(rows // 8, 8, LANES) * weights[None]).reshape(rows, LANES)


def lane_row(w_ref, row):
    return jnp.broadcast_to(w_ref[row : row + 1, :], (8, LANES))


def taps_of(w_ref, start, flip):
    order = (2, 1, 0) if flip else (0, 1, 2)
    return [lane_row(w_ref, start + t) for t in order]


def weigh(w, low, mid, high):
    return spread(w[0], low) + spread(w[1], mid) + spread(w[2], high)


def by_rows(rows, work):
    def body(i, carry):
        for store in [work(i * ROWS + t) for t in range(ROWS)]:
            store()
        return carry

    lax.fori_loop(0, rows // ROWS, body, 0)


def along_z(w, around, u_ref, rows, offset):
    def work(y):
        low, mid, high = (ref[index, y].astype(F32) for ref, index in around)
        value = weigh(w, low, mid, high)

        def store():
            u_ref[y + offset] = value

        return store

    by_rows(rows, work)


def keep_layer(new, slot, ring_ref, rows):
    ref, index = new

    def work(y):
        value = ref[index, y].astype(F32)

        def store():
            ring_ref[slot, y] = value

        return store

    by_rows(rows, work)


def along_z_ring(w, new, step, ring_ref, u_ref, rows, offset):
    ref, index = new
    low, mid, high = (lax.rem(jnp.int32(step + t), jnp.int32(3)) for t in (1, 2, 0))

    def work(y):
        last = ref[index, y].astype(F32)
        value = weigh(w, ring_ref[low, y], ring_ref[mid, y], last)

        def store():
            ring_ref[high, y] = last
            u_ref[y + offset] = value

        return store

    by_rows(rows, work)


def wrap_halves(u_ref):
    u_ref[0] = pltpu.roll(u_ref[HALF], CH, 1)
    u_ref[HALF + 1] = pltpu.roll(u_ref[1], CH, 1)


def along_y(wy, u_ref, before, here, after):
    return weigh(wy, u_ref[before], u_ref[here], u_ref[after])


def along_x(wx, value, v_ref, slot):
    v_ref[slot, 8 : 8 + NG] = value
    v_ref[slot, 7:8] = value[NG - 1 :]
    v_ref[slot, 8 + NG : 9 + NG] = value[:1]
    return weigh(wx, v_ref[slot, 7 : 7 + NG], value, v_ref[slot, 9 : 9 + NG])


def silu_terms(half):
    t = jnp.tanh(half)
    product = half * t
    bump = 1.0 - t * t
    return half + product, (1.0 + t) + half * bump, bump * (1.0 - product)


def staggered(steps, groups):
    depth = len(steps)

    def turn(i, first, last):
        for n in reversed(range(first, last)):
            steps[n](i - n)

    for i in range(depth - 1):
        turn(i, 0, i + 1)

    def body(i, carry):
        turn(i, 0, depth)
        return carry

    lax.fori_loop(depth - 1, groups, body, 0)
    for i in range(groups, groups + depth - 1):
        turn(i, i - groups + 1, depth)


def part(t):
    return slice(t * NG, (t + 1) * NG)


def first_stage(refs, u_refs, work, outs, at):
    w_ref, mix_ref = refs
    (u_ref,) = u_refs
    v_ref, left_ref = work[:2]
    h_ref, m_ref, a_ref, b_ref = outs
    wy, wx = taps_of(w_ref, 3, False), taps_of(w_ref, 6, False)
    bias = w_ref[ROW_BIAS1 : ROW_BIAS1 + 1, :]

    def taps(i):
        for t in range(GROUP):
            y = i * GROUP + t
            z = y + HALF
            top = along_y(wy, u_ref, jnp.bitwise_and(y + NG - 1, NG - 1), y, y + 1)
            end = along_y(wy, u_ref, z - 1, z, jnp.bitwise_and(z + 1, NG - 1))
            left_ref[part(t), :LANES] = along_x(wx, top, v_ref, 2 * t).astype(BF16)
            left_ref[part(t), LANES:] = along_x(wx, end, v_ref, 2 * t + 1).astype(BF16)

    def mix(i):
        mixed = jnp.dot(left_ref[...], mix_ref[...], preferred_element_type=F32)
        for t in range(GROUP):
            y = i * GROUP + t
            tangent = mixed[part(t), LANES:]
            value, slope, curve = silu_terms(mixed[part(t), :LANES] + bias)
            h_ref[at, y] = value.astype(BF16)
            m_ref[at, y] = (slope * tangent).astype(BF16)
            a_ref[at, y] = curve * tangent
            b_ref[at, y] = slope

    staggered((taps, mix), HALF // GROUP)


def second_stage(refs, u_refs, work, outs, at):
    w_ref, mix_ref, back_ref = refs
    uh_ref, um_ref = u_refs
    v_ref, left_ref, next_ref = work
    rh_ref, rm_ref = outs
    wy, wx = taps_of(w_ref, 12, False), taps_of(w_ref, 15, False)
    bias = w_ref[ROW_BIAS2 : ROW_BIAS2 + 1, :]
    scale = w_ref[ROW_SCALE : ROW_SCALE + 1, :]

    def taps(i):
        for t in range(GROUP):
            y = i * GROUP + t
            sh = along_x(wx, along_y(wy, uh_ref, y, y + 1, y + 2), v_ref, 2 * t)
            sm = along_x(wx, along_y(wy, um_ref, y, y + 1, y + 2), v_ref, 2 * t + 1)
            left_ref[part(t), :LANES] = sh.astype(BF16)
            left_ref[part(t), LANES:] = sm.astype(BF16)

    def mix(i):
        mixed = jnp.dot(left_ref[...], mix_ref[...], preferred_element_type=F32)
        _, slope, curve = silu_terms(mixed[:, :LANES] + bias)
        next_ref[:, :LANES] = (slope * (0.5 * scale)).astype(BF16)
        next_ref[:, LANES:] = (curve * scale * mixed[:, LANES:]).astype(BF16)

    def back(i):
        mixed = jnp.dot(next_ref[...], back_ref[...], preferred_element_type=F32).astype(BF16)
        for t in range(GROUP):
            rh_ref[at, i * GROUP + t] = mixed[part(t), :LANES]
            rm_ref[at, i * GROUP + t] = mixed[part(t), LANES:]

    staggered((taps, mix, back), HALF // GROUP)


def third_stage(refs, u_refs, work, outs, at):
    w_ref, back_ref, a_ref, b_ref = refs
    uh_ref, um_ref = u_refs
    v_ref, left_ref = work[:2]
    (y_ref,) = outs
    wy, wx = taps_of(w_ref, 12, True), taps_of(w_ref, 15, True)
    wx_half = taps_of(w_ref, ROW_HALF, True)

    def taps(i):
        for t in range(GROUP):
            y = i * GROUP + t
            g = along_x(wx, along_y(wy, uh_ref, y, y + 1, y + 2), v_ref, 2 * t)
            dg = along_x(wx_half, along_y(wy, um_ref, y, y + 1, y + 2), v_ref, 2 * t + 1)
            left_ref[part(t), :LANES] = (a_ref[at, y] * g + b_ref[at, y] * dg).astype(BF16)

    def back(i):
        mixed = jnp.dot(left_ref[:, :LANES], back_ref[...], preferred_element_type=F32)
        for t in range(GROUP):
            y_ref[at, i * GROUP + t] = mixed[part(t)].astype(BF16)

    staggered((taps, back), HALF // GROUP)


def fourth_rows(w_ref, u_ref, v_ref, put):
    wy, wx = taps_of(w_ref, 3, True), taps_of(w_ref, 6, True)

    def body(i, carry):
        for t in range(GROUP):
            y = i * GROUP + t
            out = along_x(wx, along_y(wy, u_ref, y, y + 1, y + 2), v_ref, t)
            put(y, out.astype(BF16).astype(F32))
        return carry

    lax.fori_loop(0, HALF // GROUP, body, 0)


def fourth_stage(refs, u_refs, work, outs, at):
    def put(y, row):
        outs[0][at, y] = row

    fourth_rows(refs[0], u_refs[0], work[0], put)


STAGES = {
    "first": (first_stage, NG, (BF16, BF16, F32, F32), (0, 1), (0, False)),
    "second": (second_stage, HALF, (BF16, BF16), (0, 1), (9, False)),
    "third": (third_stage, HALF, (BF16,), (0,), (9, True)),
    "fourth": (fourth_stage, HALF, (F32,), (), (0, True)),
}


def taker(refs):
    left = list(refs)

    def take(n):
        got = left[:n]
        del left[:n]
        return got

    return take


def inner_kernel(stage, n_const, n_field, n_local, *refs):
    body, rows, kinds, _, (start, flip) = STAGES[stage]
    take = taker(refs)
    consts = take(n_const)
    fields = [take(3) for _ in range(n_field)]
    local, outs = take(n_local), take(len(kinds))
    u_refs, ring_refs = take(n_field), take(n_field)
    work = take(3)
    offset = 0 if rows == NG else 1
    wz = taps_of(consts[0], start, flip)
    inner = fields[0][1].shape[0]

    def layer(step, which, index):
        for field, u_ref, ring_ref in zip(fields, u_refs, ring_refs):
            along_z_ring(wz, (field[which], index), step, ring_ref, u_ref, rows, offset)
            if offset:
                wrap_halves(u_ref)
        body(consts + local, u_refs, work, outs, step - 2)

    def loop(step, carry):
        layer(step, 1, step - 1)
        return carry

    for (low_ref, mid_ref, _), ring_ref in zip(fields, ring_refs):
        keep_layer((low_ref, 0), 0, ring_ref, rows)
        keep_layer((mid_ref, 0), 1, ring_ref, rows)
    lax.fori_loop(2, inner + 1, loop, 0)
    layer(inner + 1, 2, 0)


def edge_kernel(stage, n_const, n_field, n_local, places, *refs):
    body, rows, kinds, _, (start, flip) = STAGES[stage]
    take = taker(refs)
    consts = take(n_const)
    fields = [take(3) for _ in range(n_field)]
    local, outs, u_refs = take(n_local), take(len(kinds)), take(n_field)
    work = take(3)
    offset = 0 if rows == NG else 1
    wz = taps_of(consts[0], start, flip)
    for field, u_ref in zip(fields, u_refs):
        along_z(wz, list(zip(field, places)), u_ref, rows, offset)
        if offset:
            wrap_halves(u_ref)
    body(consts + local, u_refs, work, outs, 0)


def field_scratch(stage, n_field, ring):
    rows = STAGES[stage][1]
    u_rows = NG if rows == NG else HALF + 2
    scratch = [pltpu.VMEM((u_rows, NG, LANES), F32)] * n_field
    if ring:
        scratch += [pltpu.VMEM((3, rows, NG, LANES), F32)] * n_field
    left = pltpu.VMEM((GROUP * NG, 2 * LANES), BF16)
    return scratch + [pltpu.VMEM((2 * GROUP, NG + 16, LANES), F32), left, left]


def call_stage(kernel, name, layers, mib, kinds, args, scratch):
    return pl.pallas_call(
        kernel,
        out_shape=[jax.ShapeDtypeStruct((layers, HALF, NG, LANES), k) for k in kinds],
        in_specs=[vmem()] * len(args),
        out_specs=[vmem()] * len(kinds),
        scratch_shapes=scratch,
        compiler_params=params(mib),
        cost_estimate=cost(layers * 4_000_000_000, layers * 6_000_000),
        name=name,
    )(*args)


def run_inner(stage, consts, fields, local):
    kernel = functools.partial(inner_kernel, stage, len(consts), len(fields), len(local))
    args = [*consts, *[ref for field in fields for ref in field], *[x[1] for x in local]]
    scratch = field_scratch(stage, len(fields), True)
    layers = fields[0][1].shape[0]
    return call_stage(kernel, stage + "_inner", layers, 16, STAGES[stage][2], args, scratch)


def run_edge(stage, consts, fields, local, halos, side):
    inner = fields[0][1].shape[0]
    around, places = [], (0, 0, 0) if side == 0 else (inner - 1, 0, 0)
    for (low, mid, high), (below, above) in zip(fields, halos):
        around += [below, low, mid] if side == 0 else [mid, high, above]
    kernel = functools.partial(
        edge_kernel, stage, len(consts), len(fields), len(local), places
    )
    args = [*consts, *around, *[x[2 * side] for x in local]]
    scratch = field_scratch(stage, len(fields), False)
    name = stage + ("_low", "_high")[side]
    return call_stage(kernel, name, 1, 8, STAGES[stage][2], args, scratch)


def exchange(fields):
    size = lax.axis_size("slab")
    up = [(i, (i + 1) % size) for i in range(size)]
    down = [(j, i) for i, j in up]
    return [
        (lax.ppermute(high, "slab", up), lax.ppermute(low, "slab", down))
        for low, _, high in fields
    ]


def ends_kernel(w_ref, below_ref, low_ref, mid_ref, high_ref, above_ref, inner_ref, f_ref, *work):
    u_ref, v_ref = work
    inner = mid_ref.shape[0]
    layer = HALF * NG

    def copy(i, carry):
        at = pl.multiple_of(i * 256, 256)
        f_ref[pl.ds(layer + at, 256), :] = inner_ref[pl.ds(at, 256), :]
        return carry

    lax.fori_loop(0, inner * layer // 256, copy, 0)
    wz = taps_of(w_ref, 0, True)
    for base, around in (
        (0, ((below_ref, 0), (low_ref, 0), (mid_ref, 0))),
        ((inner + 1) * layer, ((mid_ref, inner - 1), (high_ref, 0), (above_ref, 0))),
    ):
        along_z(wz, around, u_ref, HALF, 1)
        wrap_halves(u_ref)

        def put(y, row, base=base):
            f_ref[pl.ds(pl.multiple_of(base + y * NG, NG), NG), :] = row

        fourth_rows(w_ref, u_ref, v_ref, put)


def run_ends(lanes, y, halos, inner):
    low, mid, high = y
    below, above = halos
    rows = (mid.shape[0] + 2) * HALF * NG
    return pl.pallas_call(
        ends_kernel,
        out_shape=jax.ShapeDtypeStruct((rows, LANES), F32),
        in_specs=[vmem()] * 7,
        out_specs=vmem(),
        scratch_shapes=[
            pltpu.VMEM((HALF + 2, NG, LANES), F32),
            pltpu.VMEM((2 * GROUP, NG + 16, LANES), F32),
        ],
        compiler_params=params(8),
        name="ends",
    )(lanes, below, low, mid, high, above, inner.reshape(-1, LANES))


def gather_kernel(spots_ref, half_ref, f_ref, out_ref, rows_ref):
    count = rows_ref.shape[0]
    unroll = 16
    eye = jnp.where(
        lax.broadcasted_iota(jnp.int32, (LANES, LANES), 0)
        == lax.broadcasted_iota(jnp.int32, (LANES, LANES), 1),
        1.0,
        0.0,
    ).astype(BF16)

    def pick(i, carry):
        for t in range(unroll):
            atom = i * unroll + t
            rows_ref[pl.ds(atom, 1), :] = f_ref[pl.ds(spots_ref[atom], 1), :]
        return carry

    lax.fori_loop(0, count // unroll, pick, 0)
    width = min(BLOCK, count)
    for start in range(0, count, width):
        at = slice(start, start + width)
        turned = lax.dot_general(
            eye,
            rows_ref[at, :].astype(BF16),
            (((1,), (1,)), ((), ())),
            preferred_element_type=F32,
        )
        later = jnp.broadcast_to(half_ref[:, at], (CH, width)) == 1
        out_ref[:, at] = jnp.where(later, turned[CH:], turned[:CH]).astype(BF16)


def make_gather(spots, half, field):
    count = spots.shape[0]
    return pl.pallas_call(
        gather_kernel,
        out_shape=jax.ShapeDtypeStruct((CH, count), BF16),
        in_specs=[smem(), vmem(), vmem()],
        out_specs=vmem(),
        scratch_shapes=[pltpu.VMEM((count, LANES), F32)],
        compiler_params=params(6),
        cost_estimate=cost(4_000_000_000, 6_000_000),
        name="gather",
    )(spots, half.reshape(1, count), field)


def finish_kernel(peers, me_ref, tab_ref, *refs):
    out_ref = refs[peers]
    me = me_ref[0]
    for j in range(peers):
        k = lax.rem(lax.bitwise_xor(me, j), NT)
        out_ref[k] = refs[j][...].astype(F32) * tab_ref[...]


def make_output(me, tab, returned):
    return pl.pallas_call(
        functools.partial(finish_kernel, len(returned)),
        out_shape=jax.ShapeDtypeStruct((NT,) + tab.shape, F32),
        in_specs=[smem()] + [vmem()] * (len(returned) + 1),
        out_specs=vmem(),
        compiler_params=params(8),
        name="finish",
    )(me, tab, *returned)


def swap(array, j):
    if j == 0:
        return array
    size = lax.axis_size("brick")
    return lax.ppermute(array, "brick", [(i, i ^ j) for i in range(size)])


def shards(
    features,
    tangents,
    route,
    cell_local,
    stencil,
    stencil_table,
    taps1,
    taps2,
    point1,
    point2,
    bias1,
    bias2,
    readout,
):
    bricks = lax.axis_size("brick")
    depth = NG // lax.axis_size("slab")
    width = NG // bricks
    me = lax.axis_index("brick").astype(jnp.int32)
    mine = me.reshape(1)

    tab, *blocks = make_deposits(mine, features, tangents, stencil, stencil_table, bricks)
    blocks, point1, route, cell_local = lax.optimization_barrier(
        (blocks, point1, route, cell_local)
    )
    mix1, mix2, back2, back1, lanes = make_weights(
        point1, point2, taps1, taps2, bias1, bias2, readout
    )
    z_part = cell_local // (width * NG)
    y_part = route[:, 0] * width + (cell_local // NG) % width
    x_part = cell_local % NG
    cell = (z_part * NG + y_part) * NG + x_part

    chunks, cells = [blocks[0]], [cell]
    (sums,) = run_scatter(first_sums_kernel, "own_sums", cells, chunks, None, depth)
    for j in range(1, bricks):
        block = blocks[j]
        if j >= 3:
            chunks[j - 2], block = lax.optimization_barrier((chunks[j - 2], block))
            cells[j - 2], cell = lax.optimization_barrier((cells[j - 2], cell))
        chunks.append(swap(block, j))
        cells.append(swap(cell, j))
    (sums,) = run_scatter(more_sums_kernel, "more_sums", cells[1:-1], chunks[1:-1], sums, depth)
    _, *charge = run_scatter(charge_kernel, "charge", cells[-1:], chunks[-1:], sums, depth)

    def both(stage, consts, fields, local, halos):
        middle = run_inner(stage, consts, fields, local)
        lows = run_edge(stage, consts, fields, local, halos, 0)
        highs = run_edge(stage, consts, fields, local, halos, 1)
        return list(zip(lows, middle, highs))

    h, m, bend, slope = both("first", [lanes, mix1], [charge], [], exchange([charge]))
    rh, rm = both("second", [lanes, mix2, back2], [h, m], [], exchange([h, m]))
    (y,) = both("third", [lanes, back1], [rh, rm], [bend, slope], exchange([rh, rm]))
    ((below, above),) = exchange([y])
    (inner,) = run_inner("fourth", [lanes], [y], [])

    field = run_ends(lanes, y, (below, above), inner)
    returned = [None] * NT
    for j in (*range(NT - 1, 0, -1), 0):
        y_of = (cells[j] // NG) % NG
        spots = ((cells[j] // (NG * NG)) * HALF + y_of % HALF) * NG + cells[j] % NG
        returned[j] = swap(make_gather(spots, y_of // HALF, field), j)
    return make_output(mine, tab, returned)


def solution(mesh):
    placed = (
        P(None, ("slab", "brick")),
        P(None, None, ("slab", "brick")),
        P(("slab", "brick"), None),
        P(("slab", "brick")),
        P(("slab", "brick")),
        P(),
        P(),
        P(),
        P(),
        P(),
        P(),
        P(),
        P(),
    )
    return jax.shard_map(
        shards,
        mesh=mesh,
        in_specs=placed,
        out_specs=P(None, None, ("slab", "brick")),
        check_vma=False,
    )
```

```python
import functools

import jax
import jax.numpy as jnp
from jax import lax
from jax.experimental import pallas as pl
from jax.experimental.pallas import tpu as pltpu
from jax.sharding import PartitionSpec as P

NG = 64
CH = 64
NT = 4
KSETS = 8
LANES = 2 * CH
HALF = NG // 2
GROUP = 8
ROWS = 4
RUN = 16
BLOCK = 256
MIB = 1024 * 1024
F32 = jnp.float32
BF16 = jnp.bfloat16


def params(mib):
    return pltpu.CompilerParams(vmem_limit_bytes=mib * MIB)


def cost(flops, nbytes):
    return pl.CostEstimate(flops=flops, bytes_accessed=nbytes, transcendentals=0)


def vmem():
    return pl.BlockSpec(memory_space=pltpu.VMEM)


def smem():
    return pl.BlockSpec(memory_space=pltpu.SMEM)


def deposits_kernel(peers, width, me_ref, feat_ref, tan_ref, sten_ref, table_ref, route_ref, local_ref, *refs):
    tab_ref, cell_ref = refs[:2]
    outs = refs[2 : peers + 2]
    feat, tan, sten, rows, route, local, sems, small = refs[peers + 2 :]
    me = me_ref[0]
    parts, _, step = feat.shape
    lists = [
        pltpu.make_async_copy(far, near, small.at[n])
        for n, (far, near) in enumerate(
            ((sten_ref, sten), (table_ref, rows), (route_ref, route), (local_ref, local))
        )
    ]
    for copy in lists:
        copy.start()
    copies = []
    for p in range(parts):
        at = pl.ds(p * step, step)
        pair = (
            pltpu.make_async_copy(feat_ref.at[:, at], feat.at[p], sems.at[p, 0]),
            pltpu.make_async_copy(tan_ref.at[:, :, at], tan.at[p], sems.at[p, 1]),
        )
        for copy in pair:
            copy.start()
        copies.append(pair)
    for copy in lists:
        copy.wait()
    place = local[...]
    z_part = lax.shift_right_logical(place, (width * NG).bit_length() - 1)
    y_part = lax.shift_right_logical(place, NG.bit_length() - 1) & (width - 1)
    cell_ref[...] = (z_part * NG + route[...] * width + y_part) * NG + (place & (NG - 1))
    table = rows[...].T
    for p in range(parts):
        at = pl.ds(p * step, step)
        kinds = jnp.broadcast_to(sten[:, at], (CH, step))
        tab = jnp.zeros((CH, step), F32)
        for s in range(KSETS):
            tab = jnp.where(kinds == s, table[:, s : s + 1], tab)
        tab_ref[:, at] = tab
        for copy in copies[p]:
            copy.wait()
        first = (feat[p].astype(F32) * tab).astype(BF16)
        for j in range(peers):
            outs[j][:CH, at] = first
            own = tan[p, lax.rem(lax.bitwise_xor(me, j), NT)]
            outs[j][CH:, at] = (own.astype(F32) * tab).astype(BF16)


def make_deposits(me, features, tangents, stencil, table, route, local, peers):
    count = features.shape[1]
    step = min(512, count)
    parts = count // step
    far = pl.BlockSpec(memory_space=pltpu.HBM)
    row = jax.ShapeDtypeStruct((1, count), jnp.int32)
    out_shape = [jax.ShapeDtypeStruct((CH, count), F32), row]
    out_shape += [jax.ShapeDtypeStruct((LANES, count), BF16)] * peers
    near_row = pltpu.VMEM((1, count), jnp.int32)
    return pl.pallas_call(
        functools.partial(deposits_kernel, peers, NG // peers),
        out_shape=out_shape,
        in_specs=[smem()] + [far] * 6,
        out_specs=[vmem()] * (peers + 2),
        scratch_shapes=[
            pltpu.VMEM((parts, CH, step), BF16),
            pltpu.VMEM((parts, NT, CH, step), BF16),
            near_row,
            pltpu.VMEM(table.shape, F32),
            near_row,
            near_row,
            pltpu.SemaphoreType.DMA((parts, 2)),
            pltpu.SemaphoreType.DMA((4,)),
        ],
        compiler_params=params(63),
        name="deposits",
    )(me, features, tangents, stencil.reshape(1, count), table, route.reshape(1, count), local.reshape(1, count))


def clear(ref):
    def body(i, carry):
        at = pl.ds(pl.multiple_of(i * 256, 256), 256)
        ref[at, :] = jnp.zeros((256, LANES), F32)
        return carry

    lax.fori_loop(0, ref.shape[0] // 256, body, 0)


def scatter(cells, chunks, marks, sums_ref, rows_ref, early_ref):
    width = early_ref.shape[0]
    blocks = rows_ref.shape[0] // width
    row = lax.broadcasted_iota(jnp.int32, (width, width), 0)
    column = lax.broadcasted_iota(jnp.int32, (width, width), 1)
    early = (column <= row) & (row // RUN == column // RUN)
    early_ref[...] = jnp.where(early, 1.0, 0.0)
    for cell_ref, chunk_ref, mark_ref in zip(cells, chunks, marks):

        def turn(i, carry):
            at = pl.ds(pl.multiple_of(i * width, width), width)
            here = jnp.broadcast_to(mark_ref[:, at].astype(F32), (width, width))
            taken = jnp.where(here.T == here, early_ref[...], 0.0).astype(BF16)
            rows_ref[at, :] = lax.dot_general(
                taken, chunk_ref[:, at], (((1,), (1,)), ((), ())), preferred_element_type=F32
            )
            return carry

        lax.fori_loop(0, blocks, turn, 0, unroll=2)

        def add(i, carry):
            first = i * RUN
            where = [cell_ref[first + t] for t in range(RUN)]
            sums = [
                sums_ref[pl.ds(cell, 1), :] + rows_ref[pl.ds(first + t, 1), :]
                for t, cell in enumerate(where)
            ]
            for cell, value in zip(where, sums):
                sums_ref[pl.ds(cell, 1), :] = value
            return carry

        lax.fori_loop(0, blocks * width // RUN, add, 0)


def split_scatter(peers, refs):
    cells, chunks = refs[:peers], refs[peers : 2 * peers]
    return cells, chunks, refs[2 * peers : 3 * peers], refs[3 * peers :]


def first_sums_kernel(peers, *refs):
    cells, chunks, marks, (sums_ref, rows_ref, early_ref) = split_scatter(peers, refs)
    clear(sums_ref)
    scatter(cells, chunks, marks, sums_ref, rows_ref, early_ref)


def more_sums_kernel(peers, *refs):
    cells, chunks, marks, (_, sums_ref, rows_ref, early_ref) = split_scatter(peers, refs)
    scatter(cells, chunks, marks, sums_ref, rows_ref, early_ref)


def round_layer(sums_ref, layer, out_ref, index):
    def body(y, carry):
        at = pl.ds(pl.multiple_of((layer * NG + y) * NG, NG), NG)
        out_ref[index, y] = sums_ref[at, :].astype(BF16)
        return carry

    lax.fori_loop(0, NG, body, 0, unroll=4)


def charge_kernel(peers, *refs):
    cells, chunks, marks, rest = split_scatter(peers, refs)
    _, sums_ref, low_ref, high_ref, rows_ref, early_ref = rest
    scatter(cells, chunks, marks, sums_ref, rows_ref, early_ref)
    round_layer(sums_ref, 0, low_ref, 0)
    round_layer(sums_ref, sums_ref.shape[0] // (NG * NG) - 1, high_ref, 0)


def inner_charge_kernel(sums_ref, mid_ref):
    def body(z, carry):
        round_layer(sums_ref, z + 1, mid_ref, z)
        return carry

    lax.fori_loop(0, mid_ref.shape[0], body, 0)


def inner_charge(sums, depth):
    return pl.pallas_call(
        inner_charge_kernel,
        out_shape=jax.ShapeDtypeStruct((depth - 2, NG, NG, LANES), BF16),
        in_specs=[vmem()],
        out_specs=vmem(),
        compiler_params=params(4),
        cost_estimate=cost(500_000_000, 600_000),
        name="inner_charge",
    )(sums)


def run_scatter(kernel, name, cells, chunks, sums, depth):
    peers, count = len(cells), cells[0].shape[0]
    width = min(BLOCK, count)
    args = [*cells, *chunks, *[c.reshape(1, count) for c in cells]]
    specs = [smem()] * peers + [vmem()] * (2 * peers)
    out_shape = [jax.ShapeDtypeStruct((depth * NG * NG, LANES), F32)]
    aliases = {}
    if sums is not None:
        aliases[len(args)] = 0
        args.append(sums)
        specs.append(vmem())
    if kernel is charge_kernel:
        out_shape += [jax.ShapeDtypeStruct((n, NG, NG, LANES), BF16) for n in (1, 1)]
    return pl.pallas_call(
        functools.partial(kernel, peers),
        out_shape=out_shape,
        in_specs=specs,
        out_specs=[vmem()] * len(out_shape),
        scratch_shapes=[pltpu.VMEM((count, LANES), F32), pltpu.VMEM((width, width), F32)],
        input_output_aliases=aliases,
        compiler_params=params(6),
        cost_estimate=cost(peers * 500_000_000, peers * 800_000),
        name=name,
    )(*args)


ROW_BIAS1, ROW_BIAS2, ROW_SCALE, ROW_HALF = 18, 19, 20, 21


def weights_kernel(p1_ref, p2_ref, t1_ref, t2_ref, b1_ref, b2_ref, r_ref, *outs):
    mix1_ref, mix2_ref, back2_ref, back1_ref, lanes_ref = outs
    p1, p2 = p1_ref[...].astype(F32), p2_ref[...].astype(F32)
    p1t, p2t = 0.5 * p1.T, 0.5 * p2.T
    zero = jnp.zeros((CH, CH), F32)

    def fill(ref, block, order):
        for i, place in enumerate(order):
            parts = [block if j == place else zero for j in range(len(order))]
            ref[i * CH : (i + 1) * CH, :] = jnp.concatenate(parts, 1).astype(BF16)

    fill(mix1_ref, p1t, (0, 2, 1, 3))
    fill(mix2_ref, p2t, (0, 1, 2, 3))
    fill(back2_ref, p2, (0, 1, 2, 3))
    fill(back1_ref, p1, (0, 1))

    def put(row, value):
        lanes_ref[row : row + 1, :] = jnp.concatenate([value, value], 1)

    for axis in range(3):
        for t in range(3):
            put(3 * axis + t, t1_ref[axis, t : t + 1, :])
            put(9 + 3 * axis + t, t2_ref[axis, t : t + 1, :])
    for t in range(3):
        put(ROW_HALF + t, 0.5 * t2_ref[2, t : t + 1, :])
    put(ROW_BIAS1, 0.5 * b1_ref[...])
    put(ROW_BIAS2, 0.5 * b2_ref[...])
    put(ROW_SCALE, r_ref[...])


def make_weights(point1, point2, taps1, taps2, bias1, bias2, readout):
    wide = jax.ShapeDtypeStruct((2 * LANES, 2 * LANES), BF16)
    return pl.pallas_call(
        weights_kernel,
        out_shape=[
            wide,
            wide,
            wide,
            jax.ShapeDtypeStruct((LANES, LANES), BF16),
            jax.ShapeDtypeStruct((24, LANES), F32),
        ],
        in_specs=[vmem()] * 7,
        out_specs=[vmem()] * 5,
        compiler_params=params(4),
        name="weights",
    )(point1, point2, taps1, taps2, *[v.reshape(1, CH) for v in (bias1, bias2, readout)])


def spread(weights, value):
    rows = value.shape[0]
    return (value.reshape(rows // 8, 8, LANES) * weights[None]).reshape(rows, LANES)


def lane_row(w_ref, row):
    return jnp.broadcast_to(w_ref[row : row + 1, :], (8, LANES))


def taps_of(w_ref, start, flip):
    order = (2, 1, 0) if flip else (0, 1, 2)
    return [lane_row(w_ref, start + t) for t in order]


def weigh(w, low, mid, high):
    return spread(w[0], low) + spread(w[1], mid) + spread(w[2], high)


def by_rows(rows, work):
    def body(i, carry):
        for store in [work(i * ROWS + t) for t in range(ROWS)]:
            store()
        return carry

    lax.fori_loop(0, rows // ROWS, body, 0)


def along_z(w, around, u_ref, rows, offset):
    def work(y):
        low, mid, high = (ref[index, y].astype(F32) for ref, index in around)
        value = weigh(w, low, mid, high)

        def store():
            u_ref[y + offset] = value

        return store

    by_rows(rows, work)


def keep_layer(new, slot, ring_ref, rows):
    ref, index = new

    def work(y):
        value = ref[index, y].astype(F32)

        def store():
            ring_ref[slot, y] = value

        return store

    by_rows(rows, work)


def along_z_ring(w, new, step, ring_ref, u_ref, rows, offset):
    ref, index = new
    low, mid, high = (lax.rem(jnp.int32(step + t), jnp.int32(3)) for t in (1, 2, 0))

    def work(y):
        last = ref[index, y].astype(F32)
        value = weigh(w, ring_ref[low, y], ring_ref[mid, y], last)

        def store():
            ring_ref[high, y] = last
            u_ref[y + offset] = value

        return store

    by_rows(rows, work)


def wrap_halves(u_ref):
    u_ref[0] = pltpu.roll(u_ref[HALF], CH, 1)
    u_ref[HALF + 1] = pltpu.roll(u_ref[1], CH, 1)


def along_y(wy, u_ref, before, here, after):
    return weigh(wy, u_ref[before], u_ref[here], u_ref[after])


def along_x(wx, value, v_ref, slot):
    v_ref[slot, 8 : 8 + NG] = value
    v_ref[slot, 7:8] = value[NG - 1 :]
    v_ref[slot, 8 + NG : 9 + NG] = value[:1]
    return weigh(wx, v_ref[slot, 7 : 7 + NG], value, v_ref[slot, 9 : 9 + NG])


def silu_terms(half):
    t = jnp.tanh(half)
    product = half * t
    bump = 1.0 - t * t
    return half + product, (1.0 + t) + half * bump, bump * (1.0 - product)


def staggered(steps, groups):
    depth = len(steps)

    def turn(i, first, last):
        for n in reversed(range(first, last)):
            steps[n](i - n, 0)

    for i in range(depth - 1):
        turn(i, 0, i + 1)

    def body(i, carry):
        turn(i, 0, depth)
        return carry

    lax.fori_loop(depth - 1, groups, body, 0)
    for i in range(groups, groups + depth - 1):
        turn(i, i - groups + 1, depth)


def staggered_layer(steps, groups, layer, final):
    depth = len(steps)

    def turn(i, first):
        for n in reversed(range(first, depth)):
            group = jnp.maximum(i - n, 0)
            steps[n](lax.rem(group, groups), lax.div(group, groups))

    def body(i, carry):
        turn(layer * groups + i, 0)
        return carry

    lax.fori_loop(0, groups, body, 0)
    if final:
        for n in range(1, depth):
            turn(jnp.int32((layer + 1) * groups + n - 1), n)


def part(t):
    return slice(t * NG, (t + 1) * NG)


def first_stage(refs, u_refs, work, outs):
    w_ref, mix_ref = refs
    (u_ref,) = u_refs
    v_ref, left_ref = work[:2]
    h_ref, m_ref, a_ref, b_ref = outs
    wy, wx = taps_of(w_ref, 3, False), taps_of(w_ref, 6, False)
    bias = w_ref[ROW_BIAS1 : ROW_BIAS1 + 1, :]

    def taps(i, at):
        for t in range(GROUP):
            y = i * GROUP + t
            z = y + HALF
            top = along_y(wy, u_ref, jnp.bitwise_and(y + NG - 1, NG - 1), y, y + 1)
            end = along_y(wy, u_ref, z - 1, z, jnp.bitwise_and(z + 1, NG - 1))
            left_ref[part(t), :LANES] = along_x(wx, top, v_ref, 2 * t).astype(BF16)
            left_ref[part(t), LANES:] = along_x(wx, end, v_ref, 2 * t + 1).astype(BF16)

    def mix(i, at):
        mixed = jnp.dot(left_ref[...], mix_ref[...], preferred_element_type=F32)
        for t in range(GROUP):
            y = i * GROUP + t
            tangent = mixed[part(t), LANES:]
            value, slope, curve = silu_terms(mixed[part(t), :LANES] + bias)
            h_ref[at, y] = value.astype(BF16)
            m_ref[at, y] = (slope * tangent).astype(BF16)
            a_ref[at, y] = curve * tangent
            b_ref[at, y] = slope

    return taps, mix


def second_stage(refs, u_refs, work, outs):
    w_ref, mix_ref, back_ref = refs
    uh_ref, um_ref = u_refs
    v_ref, left_ref, next_ref = work
    rh_ref, rm_ref = outs
    wy, wx = taps_of(w_ref, 12, False), taps_of(w_ref, 15, False)
    bias = w_ref[ROW_BIAS2 : ROW_BIAS2 + 1, :]
    scale = w_ref[ROW_SCALE : ROW_SCALE + 1, :]

    def taps(i, at):
        for t in range(GROUP):
            y = i * GROUP + t
            sh = along_x(wx, along_y(wy, uh_ref, y, y + 1, y + 2), v_ref, 2 * t)
            sm = along_x(wx, along_y(wy, um_ref, y, y + 1, y + 2), v_ref, 2 * t + 1)
            left_ref[part(t), :LANES] = sh.astype(BF16)
            left_ref[part(t), LANES:] = sm.astype(BF16)

    def mix(i, at):
        mixed = jnp.dot(left_ref[...], mix_ref[...], preferred_element_type=F32)
        _, slope, curve = silu_terms(mixed[:, :LANES] + bias)
        next_ref[:, :LANES] = (slope * (0.5 * scale)).astype(BF16)
        next_ref[:, LANES:] = (curve * scale * mixed[:, LANES:]).astype(BF16)

    def back(i, at):
        mixed = jnp.dot(next_ref[...], back_ref[...], preferred_element_type=F32).astype(BF16)
        for t in range(GROUP):
            rh_ref[at, i * GROUP + t] = mixed[part(t), :LANES]
            rm_ref[at, i * GROUP + t] = mixed[part(t), LANES:]

    return taps, mix, back


def third_stage(refs, u_refs, work, outs):
    w_ref, back_ref, a_ref, b_ref = refs
    uh_ref, um_ref = u_refs
    v_ref, left_ref = work[:2]
    (y_ref,) = outs
    wy, wx = taps_of(w_ref, 12, True), taps_of(w_ref, 15, True)
    wx_half = taps_of(w_ref, ROW_HALF, True)

    def taps(i, at):
        for t in range(GROUP):
            y = i * GROUP + t
            g = along_x(wx, along_y(wy, uh_ref, y, y + 1, y + 2), v_ref, 2 * t)
            dg = along_x(wx_half, along_y(wy, um_ref, y, y + 1, y + 2), v_ref, 2 * t + 1)
            left_ref[part(t), :LANES] = (a_ref[at, y] * g + b_ref[at, y] * dg).astype(BF16)

    def back(i, at):
        mixed = jnp.dot(left_ref[:, :LANES], back_ref[...], preferred_element_type=F32)
        for t in range(GROUP):
            y_ref[at, i * GROUP + t] = mixed[part(t)].astype(BF16)

    return taps, back


def fourth_stage(refs, u_refs, work, outs):
    (w_ref,) = refs
    (u_ref,) = u_refs
    v_ref = work[0]
    (f_ref,) = outs
    wy, wx = taps_of(w_ref, 3, True), taps_of(w_ref, 6, True)

    def taps(i, at):
        for t in range(GROUP):
            y = i * GROUP + t
            out = along_x(wx, along_y(wy, u_ref, y, y + 1, y + 2), v_ref, t)
            f_ref[at, y] = out.astype(BF16).astype(F32)

    return (taps,)


STAGES = {
    "first": (first_stage, NG, (BF16, BF16, F32, F32), (0, 1), (0, False)),
    "second": (second_stage, HALF, (BF16, BF16), (0, 1), (9, False)),
    "third": (third_stage, HALF, (BF16,), (0,), (9, True)),
    "fourth": (fourth_stage, HALF, (F32,), (), (0, True)),
}


def taker(refs):
    left = list(refs)

    def take(n):
        got = left[:n]
        del left[:n]
        return got

    return take


def inner_kernel(stage, n_const, n_field, n_local, *refs):
    body, rows, kinds, _, (start, flip) = STAGES[stage]
    take = taker(refs)
    consts = take(n_const)
    fields = [take(3) for _ in range(n_field)]
    local, outs = take(n_local), take(len(kinds))
    u_refs, ring_refs = take(n_field), take(n_field)
    work = take(3)
    offset = 0 if rows == NG else 1
    wz = taps_of(consts[0], start, flip)
    inner = fields[0][1].shape[0]
    if stage == "fourth":
        outs = [outs[0].at[pl.ds(1, inner)]]
    steps = body(consts + local, u_refs, work, outs)

    def layer(step, which, index, final):
        for field, u_ref, ring_ref in zip(fields, u_refs, ring_refs):
            along_z_ring(wz, (field[which], index), step, ring_ref, u_ref, rows, offset)
            if offset:
                wrap_halves(u_ref)
        staggered_layer(steps, HALF // GROUP, step - 2, final)

    def loop(step, carry):
        layer(step, 1, step - 1, False)
        return carry

    for (low_ref, mid_ref, _), ring_ref in zip(fields, ring_refs):
        keep_layer((low_ref, 0), 0, ring_ref, rows)
        keep_layer((mid_ref, 0), 1, ring_ref, rows)
    lax.fori_loop(2, inner + 1, loop, 0)
    layer(inner + 1, 2, 0, True)


def edge_kernel(stage, n_const, n_field, n_local, places, *refs):
    body, rows, kinds, _, (start, flip) = STAGES[stage]
    take = taker(refs)
    consts = take(n_const)
    fields = [take(3) for _ in range(n_field)]
    local, outs, u_refs = take(n_local), take(len(kinds)), take(n_field)
    work = take(3)
    offset = 0 if rows == NG else 1
    wz = taps_of(consts[0], start, flip)
    for field, u_ref in zip(fields, u_refs):
        along_z(wz, list(zip(field, places)), u_ref, rows, offset)
        if offset:
            wrap_halves(u_ref)
    staggered(body(consts + local, u_refs, work, outs), HALF // GROUP)


def field_scratch(stage, n_field, ring):
    rows = STAGES[stage][1]
    u_rows = NG if rows == NG else HALF + 2
    scratch = [pltpu.VMEM((u_rows, NG, LANES), F32)] * n_field
    if ring:
        scratch += [pltpu.VMEM((3, rows, NG, LANES), F32)] * n_field
    left = pltpu.VMEM((GROUP * NG, 2 * LANES), BF16)
    return scratch + [pltpu.VMEM((2 * GROUP, NG + 16, LANES), F32), left, left]


def call_stage(kernel, name, layers, mib, kinds, args, scratch):
    return pl.pallas_call(
        kernel,
        out_shape=[jax.ShapeDtypeStruct((layers, HALF, NG, LANES), k) for k in kinds],
        in_specs=[vmem()] * len(args),
        out_specs=[vmem()] * len(kinds),
        scratch_shapes=scratch,
        compiler_params=params(mib),
        cost_estimate=cost(layers * 4_000_000_000, layers * 6_000_000),
        name=name,
    )(*args)


def run_inner(stage, consts, fields, local):
    kernel = functools.partial(inner_kernel, stage, len(consts), len(fields), len(local))
    args = [*consts, *[ref for field in fields for ref in field], *[x[1] for x in local]]
    scratch = field_scratch(stage, len(fields), True)
    layers = fields[0][1].shape[0]
    if stage == "fourth":
        layers += 2
    return call_stage(kernel, stage + "_inner", layers, 16, STAGES[stage][2], args, scratch)


def run_edge(stage, consts, fields, local, halos, side):
    last = fields[0][1].shape[0] - 1
    around, places = [], (0, 0, 0) if side == 0 else (last, 0, 0)
    for (low, mid, high), (below, above) in zip(fields, halos):
        around += [below, low, mid] if side == 0 else [mid, high, above]
    kernel = functools.partial(
        edge_kernel, stage, len(consts), len(fields), len(local), places
    )
    args = [*consts, *around, *[x[2 * side] for x in local]]
    scratch = field_scratch(stage, len(fields), False)
    name = stage + ("_low", "_high")[side]
    return call_stage(kernel, name, 1, 8, STAGES[stage][2], args, scratch)


def exchange(fields):
    size = lax.axis_size("slab")
    up = [(i, (i + 1) % size) for i in range(size)]
    down = [(j, i) for i, j in up]
    return [
        (lax.ppermute(high, "slab", up), lax.ppermute(low, "slab", down))
        for low, _, high in fields
    ]


def ends_kernel(w_ref, below_ref, low_ref, mid_ref, high_ref, above_ref, _, f_ref, *scratch):
    u_ref, *work = scratch
    inner = mid_ref.shape[0]
    wz = taps_of(w_ref, 0, True)
    for at, around in (
        (0, ((below_ref, 0), (low_ref, 0), (mid_ref, 0))),
        (inner + 1, ((mid_ref, inner - 1), (high_ref, 0), (above_ref, 0))),
    ):
        along_z(wz, around, u_ref, HALF, 1)
        wrap_halves(u_ref)
        out = [f_ref.at[pl.ds(at, 1)]]
        staggered(fourth_stage((w_ref,), (u_ref,), work, out), HALF // GROUP)


def run_ends(lanes, y, halos, field):
    low, mid, high = y
    below, above = halos
    return pl.pallas_call(
        ends_kernel,
        out_shape=jax.ShapeDtypeStruct(field.shape, F32),
        in_specs=[vmem()] * 7,
        out_specs=vmem(),
        scratch_shapes=field_scratch("fourth", 1, False),
        input_output_aliases={6: 0},
        compiler_params=params(8),
        name="ends",
    )(lanes, below, low, mid, high, above, field)


def gather_kernel(spots_ref, half_ref, f_ref, out_ref, rows_ref):
    count = rows_ref.shape[0]
    unroll = 16
    eye = jnp.where(
        lax.broadcasted_iota(jnp.int32, (LANES, LANES), 0)
        == lax.broadcasted_iota(jnp.int32, (LANES, LANES), 1),
        1.0,
        0.0,
    ).astype(BF16)

    def pick(i, carry):
        for t in range(unroll):
            atom = i * unroll + t
            rows_ref[pl.ds(atom, 1), :] = f_ref[pl.ds(spots_ref[atom], 1), :]
        return carry

    lax.fori_loop(0, count // unroll, pick, 0)
    width = min(BLOCK, count)
    for start in range(0, count, width):
        at = slice(start, start + width)
        turned = lax.dot_general(
            eye,
            rows_ref[at, :].astype(BF16),
            (((1,), (1,)), ((), ())),
            preferred_element_type=F32,
        )
        later = jnp.broadcast_to(half_ref[:, at], (CH, width)) == 1
        out_ref[:, at] = jnp.where(later, turned[CH:], turned[:CH]).astype(BF16)


def make_gather(spots, half, field):
    count = spots.shape[0]
    return pl.pallas_call(
        gather_kernel,
        out_shape=jax.ShapeDtypeStruct((CH, count), BF16),
        in_specs=[smem(), vmem(), vmem()],
        out_specs=vmem(),
        scratch_shapes=[pltpu.VMEM((count, LANES), F32)],
        compiler_params=params(6),
        cost_estimate=cost(500_000_000, 600_000),
        name="gather",
    )(spots, half.reshape(1, count), field)


def finish_kernel(peers, me_ref, tab_ref, *refs):
    out_ref = refs[peers]
    me = me_ref[0]
    for j in range(peers):
        k = lax.rem(lax.bitwise_xor(me, j), NT)
        out_ref[k] = refs[j][...].astype(F32) * tab_ref[...]


def make_output(me, tab, returned):
    return pl.pallas_call(
        functools.partial(finish_kernel, len(returned)),
        out_shape=jax.ShapeDtypeStruct((NT,) + tab.shape, F32),
        in_specs=[smem()] + [vmem()] * (len(returned) + 1),
        out_specs=vmem(),
        compiler_params=params(8),
        name="finish",
    )(me, tab, *returned)


def swap(array, j):
    if j == 0:
        return array
    size = lax.axis_size("brick")
    return lax.ppermute(array, "brick", [(i, i ^ j) for i in range(size)])


def shards(
    features,
    tangents,
    route,
    cell_local,
    stencil,
    stencil_table,
    taps1,
    taps2,
    point1,
    point2,
    bias1,
    bias2,
    readout,
):
    bricks = lax.axis_size("brick")
    depth = NG // lax.axis_size("slab")
    me = lax.axis_index("brick").astype(jnp.int32)
    mine = me.reshape(1)

    tab, cell, *blocks = make_deposits(
        mine, features, tangents, stencil, stencil_table, route, cell_local, bricks
    )
    cell = cell.reshape(-1)
    chunks, cells = [blocks[0]], [cell]
    for j in range(1, bricks):
        block = blocks[j]
        if j == 3:
            (sums,) = run_scatter(first_sums_kernel, "own_sums", cells[:1], chunks[:1], None, depth)
            sums, point1 = lax.optimization_barrier((sums, point1))
        if j >= 3:
            sums, cell, block = lax.optimization_barrier((sums, cell, block))
        cells.append(swap(cell, j))
        chunks.append(swap(block, j))
    mix1, mix2, back2, back1, lanes = make_weights(
        point1, point2, taps1, taps2, bias1, bias2, readout
    )
    (sums,) = run_scatter(more_sums_kernel, "more_sums", cells[1:-1], chunks[1:-1], sums, depth)
    sums, low, high = run_scatter(charge_kernel, "charge", cells[-1:], chunks[-1:], sums, depth)
    charge = (low, inner_charge(sums, depth), high)

    def both(stage, consts, fields, local, halos):
        middle = run_inner(stage, consts, fields, local)
        lows = run_edge(stage, consts, fields, local, halos, 0)
        highs = run_edge(stage, consts, fields, local, halos, 1)
        return list(zip(lows, middle, highs))

    h, m, bend, slope = both("first", [lanes, mix1], [charge], [], exchange([charge]))
    rh, rm = both("second", [lanes, mix2, back2], [h, m], [], exchange([h, m]))
    (y,) = both("third", [lanes, back1], [rh, rm], [bend, slope], exchange([rh, rm]))
    ((below, above),) = exchange([y])
    (inner,) = run_inner("fourth", [lanes], [y], [])

    field = run_ends(lanes, y, (below, above), inner).reshape(-1, LANES)
    returned = [None] * NT
    for j in (*range(NT - 1, 0, -1), 0):
        y_of = (cells[j] // NG) % NG
        spots = ((cells[j] // (NG * NG)) * HALF + y_of % HALF) * NG + cells[j] % NG
        returned[j] = swap(make_gather(spots, y_of // HALF, field), j)
    return make_output(mine, tab, returned)


def solution(mesh):
    placed = (
        P(None, ("slab", "brick")),
        P(None, None, ("slab", "brick")),
        P(("slab", "brick"), None),
        P(("slab", "brick")),
        P(("slab", "brick")),
        P(),
        P(),
        P(),
        P(),
        P(),
        P(),
        P(),
        P(),
    )
    return jax.shard_map(
        shards,
        mesh=mesh,
        in_specs=placed,
        out_specs=P(None, None, ("slab", "brick")),
        check_vma=False,
    )
```

```python
import functools

import jax
import jax.numpy as jnp
from jax import lax
from jax.experimental import pallas as pl
from jax.experimental.pallas import tpu as pltpu
from jax.sharding import PartitionSpec as P

NG = 64
CH = 64
NT = 4
KSETS = 8
LANES = 2 * CH
HALF = NG // 2
GROUP = 8
ROWS = 8
RUN = 16
BLOCK = 256
MIB = 1024 * 1024
F32 = jnp.float32
BF16 = jnp.bfloat16


def params(mib):
    return pltpu.CompilerParams(vmem_limit_bytes=mib * MIB)


def cost(flops, nbytes):
    return pl.CostEstimate(flops=flops, bytes_accessed=nbytes, transcendentals=0)


def vmem():
    return pl.BlockSpec(memory_space=pltpu.VMEM)


def smem():
    return pl.BlockSpec(memory_space=pltpu.SMEM)


def deposits_kernel(peers, width, me_ref, feat_ref, tan_ref, sten_ref, table_ref, route_ref, local_ref, *refs):
    tab_ref, cell_ref = refs[:2]
    outs = refs[2 : peers + 2]
    feat, tan, sten, rows, route, local, sems, small = refs[peers + 2 :]
    me = me_ref[0]
    parts, _, step = feat.shape
    lists = [
        pltpu.make_async_copy(far, near, small.at[n])
        for n, (far, near) in enumerate(
            ((sten_ref, sten), (table_ref, rows), (route_ref, route), (local_ref, local))
        )
    ]
    for copy in lists:
        copy.start()
    copies = []
    for p in range(parts):
        at = pl.ds(p * step, step)
        pair = (
            pltpu.make_async_copy(feat_ref.at[:, at], feat.at[p], sems.at[p, 0]),
            pltpu.make_async_copy(tan_ref.at[:, :, at], tan.at[p], sems.at[p, 1]),
        )
        for copy in pair:
            copy.start()
        copies.append(pair)
    for copy in lists:
        copy.wait()
    place = local[...]
    z_part = lax.shift_right_logical(place, (width * NG).bit_length() - 1)
    y_part = lax.shift_right_logical(place, NG.bit_length() - 1) & (width - 1)
    cell_ref[...] = (z_part * NG + route[...] * width + y_part) * NG + (place & (NG - 1))
    table = rows[...].T
    for p in range(parts):
        at = pl.ds(p * step, step)
        kinds = jnp.broadcast_to(sten[:, at], (CH, step))
        tab = jnp.zeros((CH, step), F32)
        for s in range(KSETS):
            tab = jnp.where(kinds == s, table[:, s : s + 1], tab)
        tab_ref[:, at] = tab
        for copy in copies[p]:
            copy.wait()
        first = (feat[p].astype(F32) * tab).astype(BF16)
        for j in range(peers):
            outs[j][:CH, at] = first
            own = tan[p, lax.rem(lax.bitwise_xor(me, j), NT)]
            outs[j][CH:, at] = (own.astype(F32) * tab).astype(BF16)


def make_deposits(me, features, tangents, stencil, table, route, local, peers):
    count = features.shape[1]
    step = min(512, count)
    parts = count // step
    far = pl.BlockSpec(memory_space=pltpu.HBM)
    row = jax.ShapeDtypeStruct((1, count), jnp.int32)
    out_shape = [jax.ShapeDtypeStruct((CH, count), F32), row]
    out_shape += [jax.ShapeDtypeStruct((LANES, count), BF16)] * peers
    near_row = pltpu.VMEM((1, count), jnp.int32)
    return pl.pallas_call(
        functools.partial(deposits_kernel, peers, NG // peers),
        out_shape=out_shape,
        in_specs=[smem()] + [far] * 6,
        out_specs=[vmem()] * (peers + 2),
        scratch_shapes=[
            pltpu.VMEM((parts, CH, step), BF16),
            pltpu.VMEM((parts, NT, CH, step), BF16),
            near_row,
            pltpu.VMEM(table.shape, F32),
            near_row,
            near_row,
            pltpu.SemaphoreType.DMA((parts, 2)),
            pltpu.SemaphoreType.DMA((4,)),
        ],
        compiler_params=params(63),
        name="deposits",
    )(me, features, tangents, stencil.reshape(1, count), table, route.reshape(1, count), local.reshape(1, count))


def clear(ref):
    def body(i, carry):
        at = pl.ds(pl.multiple_of(i * 256, 256), 256)
        ref[at, :] = jnp.zeros((256, LANES), F32)
        return carry

    lax.fori_loop(0, ref.shape[0] // 256, body, 0)


def scatter(cells, chunks, marks, sums_ref, rows_ref, early_ref):
    width = early_ref.shape[0]
    blocks = rows_ref.shape[0] // width
    row = lax.broadcasted_iota(jnp.int32, (width, width), 0)
    column = lax.broadcasted_iota(jnp.int32, (width, width), 1)
    early = (column <= row) & (row // RUN == column // RUN)
    early_ref[...] = jnp.where(early, 1.0, 0.0)
    for cell_ref, chunk_ref, mark_ref in zip(cells, chunks, marks):

        def turn(i, carry):
            at = pl.ds(pl.multiple_of(i * width, width), width)
            here = jnp.broadcast_to(mark_ref[:, at].astype(F32), (width, width))
            taken = jnp.where(here.T == here, early_ref[...], 0.0).astype(BF16)
            rows_ref[at, :] = lax.dot_general(
                taken, chunk_ref[:, at], (((1,), (1,)), ((), ())), preferred_element_type=F32
            )
            return carry

        lax.fori_loop(0, blocks, turn, 0, unroll=2)

        def add(i, carry):
            first = i * RUN
            where = [cell_ref[first + t] for t in range(RUN)]
            sums = [
                sums_ref[pl.ds(cell, 1), :] + rows_ref[pl.ds(first + t, 1), :]
                for t, cell in enumerate(where)
            ]
            for cell, value in zip(where, sums):
                sums_ref[pl.ds(cell, 1), :] = value
            return carry

        lax.fori_loop(0, blocks * width // RUN, add, 0, unroll=4)


def split_scatter(peers, refs):
    cells, chunks = refs[:peers], refs[peers : 2 * peers]
    return cells, chunks, refs[2 * peers : 3 * peers], refs[3 * peers :]


def first_sums_kernel(peers, *refs):
    cells, chunks, marks, (sums_ref, rows_ref, early_ref) = split_scatter(peers, refs)
    clear(sums_ref)
    scatter(cells, chunks, marks, sums_ref, rows_ref, early_ref)


def more_sums_kernel(peers, *refs):
    cells, chunks, marks, (_, sums_ref, rows_ref, early_ref) = split_scatter(peers, refs)
    scatter(cells, chunks, marks, sums_ref, rows_ref, early_ref)


def round_layer(sums_ref, layer, out_ref, index):
    def body(y, carry):
        at = pl.ds(pl.multiple_of((layer * NG + y) * NG, NG), NG)
        out_ref[index, y] = sums_ref[at, :].astype(BF16)
        return carry

    lax.fori_loop(0, NG, body, 0, unroll=4)


def charge_kernel(peers, *refs):
    cells, chunks, marks, rest = split_scatter(peers, refs)
    _, sums_ref, low_ref, high_ref, rows_ref, early_ref = rest
    scatter(cells, chunks, marks, sums_ref, rows_ref, early_ref)
    round_layer(sums_ref, 0, low_ref, 0)
    round_layer(sums_ref, sums_ref.shape[0] // (NG * NG) - 1, high_ref, 0)


def inner_charge_kernel(sums_ref, mid_ref):
    def body(z, carry):
        round_layer(sums_ref, z + 1, mid_ref, z)
        return carry

    lax.fori_loop(0, mid_ref.shape[0], body, 0)


def inner_charge(sums, depth):
    return pl.pallas_call(
        inner_charge_kernel,
        out_shape=jax.ShapeDtypeStruct((depth - 2, NG, NG, LANES), BF16),
        in_specs=[vmem()],
        out_specs=vmem(),
        compiler_params=params(4),
        cost_estimate=cost(500_000_000, 600_000),
        name="inner_charge",
    )(sums)


def run_scatter(kernel, name, cells, chunks, sums, depth):
    peers, count = len(cells), cells[0].shape[0]
    width = min(BLOCK, count)
    args = [*cells, *chunks, *[c.reshape(1, count) for c in cells]]
    specs = [smem()] * peers + [vmem()] * (2 * peers)
    out_shape = [jax.ShapeDtypeStruct((depth * NG * NG, LANES), F32)]
    aliases = {}
    if sums is not None:
        aliases[len(args)] = 0
        args.append(sums)
        specs.append(vmem())
    if kernel is charge_kernel:
        out_shape += [jax.ShapeDtypeStruct((n, NG, NG, LANES), BF16) for n in (1, 1)]
    return pl.pallas_call(
        functools.partial(kernel, peers),
        out_shape=out_shape,
        in_specs=specs,
        out_specs=[vmem()] * len(out_shape),
        scratch_shapes=[pltpu.VMEM((count, LANES), F32), pltpu.VMEM((width, width), F32)],
        input_output_aliases=aliases,
        compiler_params=params(6),
        cost_estimate=cost(peers * 500_000_000, peers * 800_000),
        name=name,
    )(*args)


ROW_BIAS1, ROW_BIAS2, ROW_SCALE, ROW_HALF = 18, 19, 20, 21


def weights_kernel(p1_ref, p2_ref, t1_ref, t2_ref, b1_ref, b2_ref, r_ref, *outs):
    mix1_ref, mix2_ref, back2_ref, back1_ref, lanes_ref = outs
    p1, p2 = p1_ref[...].astype(F32), p2_ref[...].astype(F32)
    p1t, p2t = 0.5 * p1.T, 0.5 * p2.T
    zero = jnp.zeros((CH, CH), F32)

    def fill(ref, block, order):
        for i, place in enumerate(order):
            parts = [block if j == place else zero for j in range(len(order))]
            ref[i * CH : (i + 1) * CH, :] = jnp.concatenate(parts, 1).astype(BF16)

    fill(mix1_ref, p1t, (0, 2, 1, 3))
    fill(mix2_ref, p2t, (0, 1, 2, 3))
    fill(back2_ref, p2, (0, 1, 2, 3))
    fill(back1_ref, p1, (0, 1))

    def put(row, value):
        lanes_ref[row : row + 1, :] = jnp.concatenate([value, value], 1)

    for axis in range(3):
        for t in range(3):
            put(3 * axis + t, t1_ref[axis, t : t + 1, :])
            put(9 + 3 * axis + t, t2_ref[axis, t : t + 1, :])
    for t in range(3):
        put(ROW_HALF + t, 0.5 * t2_ref[2, t : t + 1, :])
    put(ROW_BIAS1, 0.5 * b1_ref[...])
    put(ROW_BIAS2, 0.5 * b2_ref[...])
    put(ROW_SCALE, r_ref[...])


def make_weights(point1, point2, taps1, taps2, bias1, bias2, readout):
    wide = jax.ShapeDtypeStruct((2 * LANES, 2 * LANES), BF16)
    return pl.pallas_call(
        weights_kernel,
        out_shape=[
            wide,
            wide,
            wide,
            jax.ShapeDtypeStruct((LANES, LANES), BF16),
            jax.ShapeDtypeStruct((24, LANES), F32),
        ],
        in_specs=[vmem()] * 7,
        out_specs=[vmem()] * 5,
        compiler_params=params(4),
        name="weights",
    )(point1, point2, taps1, taps2, *[v.reshape(1, CH) for v in (bias1, bias2, readout)])


def spread(weights, value):
    rows = value.shape[0]
    return (value.reshape(rows // 8, 8, LANES) * weights[None]).reshape(rows, LANES)


def lane_row(w_ref, row):
    return jnp.broadcast_to(w_ref[row : row + 1, :], (8, LANES))


def taps_of(w_ref, start, flip):
    order = (2, 1, 0) if flip else (0, 1, 2)
    return [lane_row(w_ref, start + t) for t in order]


def weigh(w, low, mid, high):
    return spread(w[0], low) + spread(w[1], mid) + spread(w[2], high)


def by_rows(rows, work):
    def body(i, carry):
        for store in [work(i * ROWS + t) for t in range(ROWS)]:
            store()
        return carry

    lax.fori_loop(0, rows // ROWS, body, 0)


def along_z(w, around, u_ref, rows, offset):
    def work(y):
        low, mid, high = (ref[index, y].astype(F32) for ref, index in around)
        value = weigh(w, low, mid, high)

        def store():
            u_ref[y + offset] = value

        return store

    by_rows(rows, work)


def keep_layer(new, slot, ring_ref, rows):
    ref, index = new

    def work(y):
        value = ref[index, y].astype(F32)

        def store():
            ring_ref[slot, y] = value

        return store

    by_rows(rows, work)


def along_z_ring(w, new, step, ring_ref, u_ref, rows, offset):
    ref, index = new
    low, mid, high = (lax.rem(jnp.int32(step + t), jnp.int32(3)) for t in (1, 2, 0))

    def work(y):
        last = ref[index, y].astype(F32)
        value = weigh(w, ring_ref[low, y], ring_ref[mid, y], last)

        def store():
            ring_ref[high, y] = last
            u_ref[y + offset] = value

        return store

    by_rows(rows, work)


def wrap_halves(u_ref):
    u_ref[0] = pltpu.roll(u_ref[HALF], CH, 1)
    u_ref[HALF + 1] = pltpu.roll(u_ref[1], CH, 1)


def along_y(wy, u_ref, before, here, after):
    return weigh(wy, u_ref[before], u_ref[here], u_ref[after])


def along_x(wx, value, v_ref, slot):
    v_ref[slot, 8 : 8 + NG] = value
    v_ref[slot, 7:8] = value[NG - 1 :]
    v_ref[slot, 8 + NG : 9 + NG] = value[:1]
    return weigh(wx, v_ref[slot, 7 : 7 + NG], value, v_ref[slot, 9 : 9 + NG])


def silu_terms(half):
    t = jnp.tanh(half)
    product = half * t
    bump = 1.0 - t * t
    return half + product, (1.0 + t) + half * bump, bump * (1.0 - product)


def staggered(steps, groups):
    depth = len(steps)

    def turn(i, first, last):
        for n in reversed(range(first, last)):
            steps[n](i - n, 0)

    for i in range(depth - 1):
        turn(i, 0, i + 1)

    def body(i, carry):
        turn(i, 0, depth)
        return carry

    lax.fori_loop(depth - 1, groups, body, 0)
    for i in range(groups, groups + depth - 1):
        turn(i, i - groups + 1, depth)


def staggered_layer(steps, groups, layer, final):
    depth = len(steps)

    def turn(i, first):
        for n in reversed(range(first, depth)):
            group = jnp.maximum(i - n, 0)
            steps[n](lax.rem(group, groups), lax.div(group, groups))

    def body(i, carry):
        turn(layer * groups + i, 0)
        return carry

    lax.fori_loop(0, groups, body, 0)
    if final:
        for n in range(1, depth):
            turn(jnp.int32((layer + 1) * groups + n - 1), n)


def part(t):
    return slice(t * NG, (t + 1) * NG)


def first_stage(refs, u_refs, work, outs):
    w_ref, mix_ref = refs
    (u_ref,) = u_refs
    v_ref, left_ref = work[:2]
    h_ref, m_ref, a_ref, b_ref = outs
    wy, wx = taps_of(w_ref, 3, False), taps_of(w_ref, 6, False)
    bias = w_ref[ROW_BIAS1 : ROW_BIAS1 + 1, :]

    def taps(i, at):
        for t in range(GROUP):
            y = i * GROUP + t
            z = y + HALF
            top = along_y(wy, u_ref, jnp.bitwise_and(y + NG - 1, NG - 1), y, y + 1)
            end = along_y(wy, u_ref, z - 1, z, jnp.bitwise_and(z + 1, NG - 1))
            left_ref[part(t), :LANES] = along_x(wx, top, v_ref, 2 * t).astype(BF16)
            left_ref[part(t), LANES:] = along_x(wx, end, v_ref, 2 * t + 1).astype(BF16)

    def mix(i, at):
        mixed = jnp.dot(left_ref[...], mix_ref[...], preferred_element_type=F32)
        for t in range(GROUP):
            y = i * GROUP + t
            tangent = mixed[part(t), LANES:]
            value, slope, curve = silu_terms(mixed[part(t), :LANES] + bias)
            h_ref[at, y] = value.astype(BF16)
            m_ref[at, y] = (slope * tangent).astype(BF16)
            a_ref[at, y] = curve * tangent
            b_ref[at, y] = slope

    return taps, mix


def second_stage(refs, u_refs, work, outs):
    w_ref, mix_ref, back_ref = refs
    uh_ref, um_ref = u_refs
    v_ref, left_ref, next_ref = work
    rh_ref, rm_ref = outs
    wy, wx = taps_of(w_ref, 12, False), taps_of(w_ref, 15, False)
    bias = w_ref[ROW_BIAS2 : ROW_BIAS2 + 1, :]
    scale = w_ref[ROW_SCALE : ROW_SCALE + 1, :]

    def taps(i, at):
        for t in range(GROUP):
            y = i * GROUP + t
            sh = along_x(wx, along_y(wy, uh_ref, y, y + 1, y + 2), v_ref, 2 * t)
            sm = along_x(wx, along_y(wy, um_ref, y, y + 1, y + 2), v_ref, 2 * t + 1)
            left_ref[part(t), :LANES] = sh.astype(BF16)
            left_ref[part(t), LANES:] = sm.astype(BF16)

    def mix(i, at):
        mixed = jnp.dot(left_ref[...], mix_ref[...], preferred_element_type=F32)
        _, slope, curve = silu_terms(mixed[:, :LANES] + bias)
        next_ref[:, :LANES] = (slope * (0.5 * scale)).astype(BF16)
        next_ref[:, LANES:] = (curve * scale * mixed[:, LANES:]).astype(BF16)

    def back(i, at):
        mixed = jnp.dot(next_ref[...], back_ref[...], preferred_element_type=F32).astype(BF16)
        for t in range(GROUP):
            rh_ref[at, i * GROUP + t] = mixed[part(t), :LANES]
            rm_ref[at, i * GROUP + t] = mixed[part(t), LANES:]

    return taps, mix, back


def third_stage(refs, u_refs, work, outs):
    w_ref, back_ref, a_ref, b_ref = refs
    uh_ref, um_ref = u_refs
    v_ref, left_ref = work[:2]
    (y_ref,) = outs
    wy, wx = taps_of(w_ref, 12, True), taps_of(w_ref, 15, True)
    wx_half = taps_of(w_ref, ROW_HALF, True)

    def taps(i, at):
        for t in range(GROUP):
            y = i * GROUP + t
            g = along_x(wx, along_y(wy, uh_ref, y, y + 1, y + 2), v_ref, 2 * t)
            dg = along_x(wx_half, along_y(wy, um_ref, y, y + 1, y + 2), v_ref, 2 * t + 1)
            left_ref[part(t), :LANES] = (a_ref[at, y] * g + b_ref[at, y] * dg).astype(BF16)

    def back(i, at):
        mixed = jnp.dot(left_ref[:, :LANES], back_ref[...], preferred_element_type=F32)
        for t in range(GROUP):
            y_ref[at, i * GROUP + t] = mixed[part(t)].astype(BF16)

    return taps, back


def fourth_stage(refs, u_refs, work, outs):
    (w_ref,) = refs
    (u_ref,) = u_refs
    v_ref = work[0]
    (f_ref,) = outs
    wy, wx = taps_of(w_ref, 3, True), taps_of(w_ref, 6, True)

    def taps(i, at):
        for t in range(GROUP):
            y = i * GROUP + t
            out = along_x(wx, along_y(wy, u_ref, y, y + 1, y + 2), v_ref, t)
            f_ref[at, y] = out.astype(BF16).astype(F32)

    return (taps,)


STAGES = {
    "first": (first_stage, NG, (BF16, BF16, F32, F32), (0, 1), (0, False)),
    "second": (second_stage, HALF, (BF16, BF16), (0, 1), (9, False)),
    "third": (third_stage, HALF, (BF16,), (0,), (9, True)),
    "fourth": (fourth_stage, HALF, (F32,), (), (0, True)),
}


def taker(refs):
    left = list(refs)

    def take(n):
        got = left[:n]
        del left[:n]
        return got

    return take


def inner_kernel(stage, n_const, n_field, n_local, *refs):
    body, rows, kinds, _, (start, flip) = STAGES[stage]
    take = taker(refs)
    consts = take(n_const)
    fields = [take(3) for _ in range(n_field)]
    local, outs = take(n_local), take(len(kinds))
    u_refs, ring_refs = take(n_field), take(n_field)
    work = take(3)
    offset = 0 if rows == NG else 1
    wz = taps_of(consts[0], start, flip)
    inner = fields[0][1].shape[0]
    if stage == "fourth":
        outs = [outs[0].at[pl.ds(1, inner)]]
    steps = body(consts + local, u_refs, work, outs)

    def layer(step, which, index, final):
        for field, u_ref, ring_ref in zip(fields, u_refs, ring_refs):
            along_z_ring(wz, (field[which], index), step, ring_ref, u_ref, rows, offset)
            if offset:
                wrap_halves(u_ref)
        staggered_layer(steps, HALF // GROUP, step - 2, final)

    def loop(step, carry):
        layer(step, 1, step - 1, False)
        return carry

    for (low_ref, mid_ref, _), ring_ref in zip(fields, ring_refs):
        keep_layer((low_ref, 0), 0, ring_ref, rows)
        keep_layer((mid_ref, 0), 1, ring_ref, rows)
    lax.fori_loop(2, inner + 1, loop, 0)
    layer(inner + 1, 2, 0, True)


def edge_kernel(stage, n_const, n_field, n_local, places, *refs):
    body, rows, kinds, _, (start, flip) = STAGES[stage]
    take = taker(refs)
    consts = take(n_const)
    fields = [take(3) for _ in range(n_field)]
    local, outs, u_refs = take(n_local), take(len(kinds)), take(n_field)
    work = take(3)
    offset = 0 if rows == NG else 1
    wz = taps_of(consts[0], start, flip)
    for field, u_ref in zip(fields, u_refs):
        along_z(wz, list(zip(field, places)), u_ref, rows, offset)
        if offset:
            wrap_halves(u_ref)
    staggered(body(consts + local, u_refs, work, outs), HALF // GROUP)


def field_scratch(stage, n_field, ring):
    rows = STAGES[stage][1]
    u_rows = NG if rows == NG else HALF + 2
    scratch = [pltpu.VMEM((u_rows, NG, LANES), F32)] * n_field
    if ring:
        scratch += [pltpu.VMEM((3, rows, NG, LANES), F32)] * n_field
    left = pltpu.VMEM((GROUP * NG, 2 * LANES), BF16)
    return scratch + [pltpu.VMEM((2 * GROUP, NG + 16, LANES), F32), left, left]


def call_stage(kernel, name, layers, mib, kinds, args, scratch):
    return pl.pallas_call(
        kernel,
        out_shape=[jax.ShapeDtypeStruct((layers, HALF, NG, LANES), k) for k in kinds],
        in_specs=[vmem()] * len(args),
        out_specs=[vmem()] * len(kinds),
        scratch_shapes=scratch,
        compiler_params=params(mib),
        cost_estimate=cost(layers * 4_000_000_000, layers * 6_000_000),
        name=name,
    )(*args)


def run_inner(stage, consts, fields, local):
    kernel = functools.partial(inner_kernel, stage, len(consts), len(fields), len(local))
    args = [*consts, *[ref for field in fields for ref in field], *[x[1] for x in local]]
    scratch = field_scratch(stage, len(fields), True)
    layers = fields[0][1].shape[0]
    if stage == "fourth":
        layers += 2
    return call_stage(kernel, stage + "_inner", layers, 16, STAGES[stage][2], args, scratch)


def run_edge(stage, consts, fields, local, halos, side):
    last = fields[0][1].shape[0] - 1
    around, places = [], (0, 0, 0) if side == 0 else (last, 0, 0)
    for (low, mid, high), (below, above) in zip(fields, halos):
        around += [below, low, mid] if side == 0 else [mid, high, above]
    kernel = functools.partial(
        edge_kernel, stage, len(consts), len(fields), len(local), places
    )
    args = [*consts, *around, *[x[2 * side] for x in local]]
    scratch = field_scratch(stage, len(fields), False)
    name = stage + ("_low", "_high")[side]
    return call_stage(kernel, name, 1, 8, STAGES[stage][2], args, scratch)


def exchange(fields):
    size = lax.axis_size("slab")
    up = [(i, (i + 1) % size) for i in range(size)]
    down = [(j, i) for i, j in up]
    return [
        (lax.ppermute(high, "slab", up), lax.ppermute(low, "slab", down))
        for low, _, high in fields
    ]


def ends_kernel(w_ref, below_ref, low_ref, mid_ref, high_ref, above_ref, _, f_ref, *scratch):
    u_ref, *work = scratch
    inner = mid_ref.shape[0]
    wz = taps_of(w_ref, 0, True)
    for at, around in (
        (0, ((below_ref, 0), (low_ref, 0), (mid_ref, 0))),
        (inner + 1, ((mid_ref, inner - 1), (high_ref, 0), (above_ref, 0))),
    ):
        along_z(wz, around, u_ref, HALF, 1)
        wrap_halves(u_ref)
        out = [f_ref.at[pl.ds(at, 1)]]
        staggered(fourth_stage((w_ref,), (u_ref,), work, out), HALF // GROUP)


def run_ends(lanes, y, halos, field):
    low, mid, high = y
    below, above = halos
    return pl.pallas_call(
        ends_kernel,
        out_shape=jax.ShapeDtypeStruct(field.shape, F32),
        in_specs=[vmem()] * 7,
        out_specs=vmem(),
        scratch_shapes=field_scratch("fourth", 1, False),
        input_output_aliases={6: 0},
        compiler_params=params(8),
        name="ends",
    )(lanes, below, low, mid, high, above, field)


def gather_kernel(spots_ref, half_ref, f_ref, out_ref, rows_ref):
    count = rows_ref.shape[0]
    unroll = 128
    eye = jnp.where(
        lax.broadcasted_iota(jnp.int32, (LANES, LANES), 0)
        == lax.broadcasted_iota(jnp.int32, (LANES, LANES), 1),
        1.0,
        0.0,
    ).astype(BF16)

    def pick(i, carry):
        for t in range(unroll):
            atom = i * unroll + t
            rows_ref[pl.ds(atom, 1), :] = f_ref[pl.ds(spots_ref[atom], 1), :]
        return carry

    lax.fori_loop(0, count // unroll, pick, 0)
    width = min(BLOCK, count)
    for start in range(0, count, width):
        at = slice(start, start + width)
        turned = lax.dot_general(
            eye,
            rows_ref[at, :].astype(BF16),
            (((1,), (1,)), ((), ())),
            preferred_element_type=F32,
        )
        later = jnp.broadcast_to(half_ref[:, at], (CH, width)) == 1
        out_ref[:, at] = jnp.where(later, turned[CH:], turned[:CH]).astype(BF16)


def make_gather(spots, half, field):
    count = spots.shape[0]
    return pl.pallas_call(
        gather_kernel,
        out_shape=jax.ShapeDtypeStruct((CH, count), BF16),
        in_specs=[smem(), vmem(), vmem()],
        out_specs=vmem(),
        scratch_shapes=[pltpu.VMEM((count, LANES), F32)],
        compiler_params=params(6),
        cost_estimate=cost(500_000_000, 600_000),
        name="gather",
    )(spots, half.reshape(1, count), field)


def finish_kernel(peers, me_ref, tab_ref, *refs):
    out_ref, rows_ref, sems = refs[-3:]
    copies = []
    for n in range(peers):
        k = lax.rem(lax.bitwise_xor(me_ref[0], n), NT)
        rows_ref[n] = refs[n][...].astype(F32) * tab_ref[...]
        copies.append(pltpu.make_async_copy(rows_ref.at[n], out_ref.at[k], sems.at[n]))
        copies[-1].start()
    for copy in copies:
        copy.wait()


def make_output(me, tab, returned):
    count = len(returned)
    return pl.pallas_call(
        functools.partial(finish_kernel, count),
        out_shape=jax.ShapeDtypeStruct((NT,) + tab.shape, F32),
        in_specs=[smem()] + [vmem()] * (count + 1),
        out_specs=pl.BlockSpec(memory_space=pl.ANY),
        scratch_shapes=[
            pltpu.VMEM((count,) + tab.shape, F32),
            pltpu.SemaphoreType.DMA((count,)),
        ],
        compiler_params=params(8),
        name="finish",
    )(me, tab, *returned)


def swap(array, j):
    if j == 0:
        return array
    size = lax.axis_size("brick")
    return lax.ppermute(array, "brick", [(i, i ^ j) for i in range(size)])


def shards(
    features,
    tangents,
    route,
    cell_local,
    stencil,
    stencil_table,
    taps1,
    taps2,
    point1,
    point2,
    bias1,
    bias2,
    readout,
):
    bricks = lax.axis_size("brick")
    depth = NG // lax.axis_size("slab")
    me = lax.axis_index("brick").astype(jnp.int32)
    mine = me.reshape(1)

    tab, cell, *blocks = make_deposits(
        mine, features, tangents, stencil, stencil_table, route, cell_local, bricks
    )
    cell = cell.reshape(-1)
    chunks, cells = [blocks[0]], [cell]
    for j in range(1, bricks):
        block = blocks[j]
        if j == 3:
            (sums,) = run_scatter(first_sums_kernel, "own_sums", cells[:1], chunks[:1], None, depth)
            sums, point1 = lax.optimization_barrier((sums, point1))
        if j >= 3:
            sums, cell, block = lax.optimization_barrier((sums, cell, block))
        cells.append(swap(cell, j))
        chunks.append(swap(block, j))
    mix1, mix2, back2, back1, lanes = make_weights(
        point1, point2, taps1, taps2, bias1, bias2, readout
    )
    (sums,) = run_scatter(more_sums_kernel, "more_sums", cells[1:-1], chunks[1:-1], sums, depth)
    sums, low, high = run_scatter(charge_kernel, "charge", cells[-1:], chunks[-1:], sums, depth)
    charge = (low, inner_charge(sums, depth), high)

    def both(stage, consts, fields, local, halos):
        middle = run_inner(stage, consts, fields, local)
        lows = run_edge(stage, consts, fields, local, halos, 0)
        highs = run_edge(stage, consts, fields, local, halos, 1)
        return list(zip(lows, middle, highs))

    h, m, bend, slope = both("first", [lanes, mix1], [charge], [], exchange([charge]))
    rh, rm = both("second", [lanes, mix2, back2], [h, m], [], exchange([h, m]))
    (y,) = both("third", [lanes, back1], [rh, rm], [bend, slope], exchange([rh, rm]))
    ((below, above),) = exchange([y])
    (inner,) = run_inner("fourth", [lanes], [y], [])

    field = run_ends(lanes, y, (below, above), inner).reshape(-1, LANES)
    returned = [None] * NT
    for j in (*range(NT - 1, 0, -1), 0):
        y_of = (cells[j] // NG) % NG
        spots = ((cells[j] // (NG * NG)) * HALF + y_of % HALF) * NG + cells[j] % NG
        returned[j] = swap(make_gather(spots, y_of // HALF, field), j)
    return make_output(mine, tab, returned)


def solution(mesh):
    placed = (
        P(None, ("slab", "brick")),
        P(None, None, ("slab", "brick")),
        P(("slab", "brick"), None),
        P(("slab", "brick")),
        P(("slab", "brick")),
        P(),
        P(),
        P(),
        P(),
        P(),
        P(),
        P(),
        P(),
    )
    return jax.shard_map(
        shards,
        mesh=mesh,
        in_specs=placed,
        out_specs=P(None, None, ("slab", "brick")),
        check_vma=False,
    )
```

```python
import functools

import jax
import jax.numpy as jnp
from jax import lax
from jax.experimental import pallas as pl
from jax.experimental.pallas import tpu as pltpu
from jax.sharding import PartitionSpec as P

NG = 64
CH = 64
NT = 4
KSETS = 8
LANES = 2 * CH
HALF = NG // 2
GROUP = 8
ROWS = 8
RUN = 16
BLOCK = 256
MIB = 1024 * 1024
F32 = jnp.float32
BF16 = jnp.bfloat16


def params(mib):
    return pltpu.CompilerParams(vmem_limit_bytes=mib * MIB)


def cost(flops, nbytes):
    return pl.CostEstimate(flops=flops, bytes_accessed=nbytes, transcendentals=0)


def vmem():
    return pl.BlockSpec(memory_space=pltpu.VMEM)


def smem():
    return pl.BlockSpec(memory_space=pltpu.SMEM)


def deposits_kernel(peers, width, me_ref, feat_ref, tan_ref, sten_ref, table_ref, route_ref, local_ref, *refs):
    tab_ref, cell_ref = refs[:2]
    outs = refs[2 : peers + 2]
    feat, tan, sten, rows, route, local, tabs, blocks, sems, small, out_sems = refs[peers + 2 :]
    me = me_ref[0]
    parts, _, step = feat.shape
    lists = [
        pltpu.make_async_copy(far, near, small.at[n])
        for n, (far, near) in enumerate(
            ((sten_ref, sten), (table_ref, rows), (route_ref, route), (local_ref, local))
        )
    ]
    for copy in lists:
        copy.start()
    copies = []
    for p in range(parts):
        at = pl.ds(p * step, step)
        pair = (
            pltpu.make_async_copy(feat_ref.at[:, at], feat.at[p], sems.at[p, 0]),
            pltpu.make_async_copy(tan_ref.at[:, :, at], tan.at[p], sems.at[p, 1]),
        )
        for copy in pair:
            copy.start()
        copies.append(pair)
    for copy in lists:
        copy.wait()
    place = local[...]
    z_part = lax.shift_right_logical(place, (width * NG).bit_length() - 1)
    y_part = lax.shift_right_logical(place, NG.bit_length() - 1) & (width - 1)
    cell_ref[...] = (z_part * NG + route[...] * width + y_part) * NG + (place & (NG - 1))
    table = rows[...].T
    sent = []
    for p in range(parts):
        at = pl.ds(p * step, step)
        kinds = jnp.broadcast_to(sten[:, at], (CH, step))
        tab = jnp.zeros((CH, step), F32)
        for s in range(KSETS):
            tab = jnp.where(kinds == s, table[:, s : s + 1], tab)
        tabs[p] = tab
        sent.append(pltpu.make_async_copy(tabs.at[p], tab_ref.at[:, at], out_sems.at[p, peers]))
        sent[-1].start()
        for copy in copies[p]:
            copy.wait()
        first = (feat[p].astype(F32) * tab).astype(BF16)
        for j in range(peers):
            blocks[p, j, :CH, :] = first
            own = tan[p, lax.rem(lax.bitwise_xor(me, j), NT)]
            blocks[p, j, CH:, :] = (own.astype(F32) * tab).astype(BF16)
            sent.append(
                pltpu.make_async_copy(blocks.at[p, j], outs[j].at[:, at], out_sems.at[p, j])
            )
            sent[-1].start()
    for copy in sent:
        copy.wait()


def make_deposits(me, features, tangents, stencil, table, route, local, peers):
    count = features.shape[1]
    step = min(512, count)
    parts = count // step
    far = pl.BlockSpec(memory_space=pltpu.HBM)
    row = jax.ShapeDtypeStruct((1, count), jnp.int32)
    out_shape = [jax.ShapeDtypeStruct((CH, count), F32), row]
    out_shape += [jax.ShapeDtypeStruct((LANES, count), BF16)] * peers
    near_row = pltpu.VMEM((1, count), jnp.int32)
    return pl.pallas_call(
        functools.partial(deposits_kernel, peers, NG // peers),
        out_shape=out_shape,
        in_specs=[smem()] + [far] * 6,
        out_specs=[far, vmem()] + [far] * peers,
        scratch_shapes=[
            pltpu.VMEM((parts, CH, step), BF16),
            pltpu.VMEM((parts, NT, CH, step), BF16),
            near_row,
            pltpu.VMEM(table.shape, F32),
            near_row,
            near_row,
            pltpu.VMEM((parts, CH, step), F32),
            pltpu.VMEM((parts, peers, LANES, step), BF16),
            pltpu.SemaphoreType.DMA((parts, 2)),
            pltpu.SemaphoreType.DMA((4,)),
            pltpu.SemaphoreType.DMA((parts, peers + 1)),
        ],
        compiler_params=params(63),
        name="deposits",
    )(me, features, tangents, stencil.reshape(1, count), table, route.reshape(1, count), local.reshape(1, count))


def clear(ref):
    def body(i, carry):
        at = pl.ds(pl.multiple_of(i * 256, 256), 256)
        ref[at, :] = jnp.zeros((256, LANES), F32)
        return carry

    lax.fori_loop(0, ref.shape[0] // 256, body, 0)


def scatter(cells, chunks, marks, sums_ref, rows_ref, early_ref):
    width = early_ref.shape[0]
    blocks = rows_ref.shape[0] // width
    row = lax.broadcasted_iota(jnp.int32, (width, width), 0)
    column = lax.broadcasted_iota(jnp.int32, (width, width), 1)
    early = (column <= row) & (row // RUN == column // RUN)
    early_ref[...] = jnp.where(early, 1.0, 0.0)
    for cell_ref, chunk_ref, mark_ref in zip(cells, chunks, marks):

        def turn(i, carry):
            at = pl.ds(pl.multiple_of(i * width, width), width)
            here = jnp.broadcast_to(mark_ref[:, at].astype(F32), (width, width))
            taken = jnp.where(here.T == here, early_ref[...], 0.0).astype(BF16)
            rows_ref[at, :] = lax.dot_general(
                taken, chunk_ref[:, at], (((1,), (1,)), ((), ())), preferred_element_type=F32
            )
            return carry

        lax.fori_loop(0, blocks, turn, 0, unroll=2)

        def add(i, carry):
            first = i * RUN
            where = [cell_ref[first + t] for t in range(RUN)]
            sums = [
                sums_ref[pl.ds(cell, 1), :] + rows_ref[pl.ds(first + t, 1), :]
                for t, cell in enumerate(where)
            ]
            for cell, value in zip(where, sums):
                sums_ref[pl.ds(cell, 1), :] = value
            return carry

        lax.fori_loop(0, blocks * width // RUN, add, 0, unroll=4)


def split_scatter(peers, refs):
    cells, chunks = refs[:peers], refs[peers : 2 * peers]
    return cells, chunks, refs[2 * peers : 3 * peers], refs[3 * peers :]


def first_sums_kernel(peers, *refs):
    cells, chunks, marks, (sums_ref, rows_ref, early_ref) = split_scatter(peers, refs)
    clear(sums_ref)
    scatter(cells, chunks, marks, sums_ref, rows_ref, early_ref)


def more_sums_kernel(peers, *refs):
    cells, chunks, marks, (_, sums_ref, rows_ref, early_ref) = split_scatter(peers, refs)
    scatter(cells, chunks, marks, sums_ref, rows_ref, early_ref)


def round_layer(sums_ref, layer, out_ref, index):
    def body(y, carry):
        at = pl.ds(pl.multiple_of((layer * NG + y) * NG, NG), NG)
        out_ref[index, y] = sums_ref[at, :].astype(BF16)
        return carry

    lax.fori_loop(0, NG, body, 0, unroll=4)


def charge_kernel(peers, *refs):
    cells, chunks, marks, rest = split_scatter(peers, refs)
    _, sums_ref, low_ref, high_ref, rows_ref, early_ref = rest
    scatter(cells, chunks, marks, sums_ref, rows_ref, early_ref)
    round_layer(sums_ref, 0, low_ref, 0)
    round_layer(sums_ref, sums_ref.shape[0] // (NG * NG) - 1, high_ref, 0)


def inner_charge_kernel(sums_ref, mid_ref):
    def body(z, carry):
        round_layer(sums_ref, z + 1, mid_ref, z)
        return carry

    lax.fori_loop(0, mid_ref.shape[0], body, 0)


def inner_charge(sums, depth):
    return pl.pallas_call(
        inner_charge_kernel,
        out_shape=jax.ShapeDtypeStruct((depth - 2, NG, NG, LANES), BF16),
        in_specs=[vmem()],
        out_specs=vmem(),
        compiler_params=params(4),
        cost_estimate=cost(500_000_000, 600_000),
        name="inner_charge",
    )(sums)


def run_scatter(kernel, name, cells, chunks, sums, depth):
    peers, count = len(cells), cells[0].shape[0]
    width = min(BLOCK, count)
    args = [*cells, *chunks, *[c.reshape(1, count) for c in cells]]
    specs = [smem()] * peers + [vmem()] * (2 * peers)
    out_shape = [jax.ShapeDtypeStruct((depth * NG * NG, LANES), F32)]
    aliases = {}
    if sums is not None:
        aliases[len(args)] = 0
        args.append(sums)
        specs.append(vmem())
    if kernel is charge_kernel:
        out_shape += [jax.ShapeDtypeStruct((n, NG, NG, LANES), BF16) for n in (1, 1)]
    return pl.pallas_call(
        functools.partial(kernel, peers),
        out_shape=out_shape,
        in_specs=specs,
        out_specs=[vmem()] * len(out_shape),
        scratch_shapes=[pltpu.VMEM((count, LANES), F32), pltpu.VMEM((width, width), F32)],
        input_output_aliases=aliases,
        compiler_params=params(6),
        cost_estimate=cost(peers * 500_000_000, peers * 800_000),
        name=name,
    )(*args)


ROW_BIAS1, ROW_BIAS2, ROW_SCALE, ROW_HALF = 18, 19, 20, 21


def weights_kernel(p1_ref, p2_ref, t1_ref, t2_ref, b1_ref, b2_ref, r_ref, *outs):
    mix1_ref, mix2_ref, back2_ref, back1_ref, lanes_ref = outs
    p1, p2 = p1_ref[...].astype(F32), p2_ref[...].astype(F32)
    p1t, p2t = 0.5 * p1.T, 0.5 * p2.T
    zero = jnp.zeros((CH, CH), F32)

    def fill(ref, block, order):
        for i, place in enumerate(order):
            parts = [block if j == place else zero for j in range(len(order))]
            ref[i * CH : (i + 1) * CH, :] = jnp.concatenate(parts, 1).astype(BF16)

    fill(mix1_ref, p1t, (0, 2, 1, 3))
    fill(mix2_ref, p2t, (0, 1, 2, 3))
    fill(back2_ref, p2, (0, 1, 2, 3))
    fill(back1_ref, p1, (0, 1))

    def put(row, value):
        lanes_ref[row : row + 1, :] = jnp.concatenate([value, value], 1)

    for axis in range(3):
        for t in range(3):
            put(3 * axis + t, t1_ref[axis, t : t + 1, :])
            put(9 + 3 * axis + t, t2_ref[axis, t : t + 1, :])
    for t in range(3):
        put(ROW_HALF + t, 0.5 * t2_ref[2, t : t + 1, :])
    put(ROW_BIAS1, 0.5 * b1_ref[...])
    put(ROW_BIAS2, 0.5 * b2_ref[...])
    put(ROW_SCALE, r_ref[...])


def make_weights(point1, point2, taps1, taps2, bias1, bias2, readout):
    wide = jax.ShapeDtypeStruct((2 * LANES, 2 * LANES), BF16)
    return pl.pallas_call(
        weights_kernel,
        out_shape=[
            wide,
            wide,
            wide,
            jax.ShapeDtypeStruct((LANES, LANES), BF16),
            jax.ShapeDtypeStruct((24, LANES), F32),
        ],
        in_specs=[vmem()] * 7,
        out_specs=[vmem()] * 5,
        compiler_params=params(4),
        name="weights",
    )(point1, point2, taps1, taps2, *[v.reshape(1, CH) for v in (bias1, bias2, readout)])


def spread(weights, value):
    rows = value.shape[0]
    return (value.reshape(rows // 8, 8, LANES) * weights[None]).reshape(rows, LANES)


def lane_row(w_ref, row):
    return jnp.broadcast_to(w_ref[row : row + 1, :], (8, LANES))


def taps_of(w_ref, start, flip):
    order = (2, 1, 0) if flip else (0, 1, 2)
    return [lane_row(w_ref, start + t) for t in order]


def weigh(w, low, mid, high):
    return spread(w[0], low) + spread(w[1], mid) + spread(w[2], high)


def by_rows(rows, work):
    def body(i, carry):
        for store in [work(i * ROWS + t) for t in range(ROWS)]:
            store()
        return carry

    lax.fori_loop(0, rows // ROWS, body, 0)


def along_z(w, around, u_ref, rows, offset):
    def work(y):
        low, mid, high = (ref[index, y].astype(F32) for ref, index in around)
        value = weigh(w, low, mid, high)

        def store():
            u_ref[y + offset] = value

        return store

    by_rows(rows, work)


def keep_layer(new, slot, ring_ref, rows):
    ref, index = new

    def work(y):
        value = ref[index, y].astype(F32)

        def store():
            ring_ref[slot, y] = value

        return store

    by_rows(rows, work)


def along_z_ring(w, new, step, ring_ref, u_ref, rows, offset):
    ref, index = new
    low, mid, high = (lax.rem(jnp.int32(step + t), jnp.int32(3)) for t in (1, 2, 0))

    def work(y):
        last = ref[index, y].astype(F32)
        value = weigh(w, ring_ref[low, y], ring_ref[mid, y], last)

        def store():
            ring_ref[high, y] = last
            u_ref[y + offset] = value

        return store

    by_rows(rows, work)


def wrap_halves(u_ref):
    u_ref[0] = pltpu.roll(u_ref[HALF], CH, 1)
    u_ref[HALF + 1] = pltpu.roll(u_ref[1], CH, 1)


def along_y(wy, u_ref, before, here, after):
    return weigh(wy, u_ref[before], u_ref[here], u_ref[after])


def along_x(wx, value, v_ref, slot):
    v_ref[slot, 8 : 8 + NG] = value
    v_ref[slot, 7:8] = value[NG - 1 :]
    v_ref[slot, 8 + NG : 9 + NG] = value[:1]
    return weigh(wx, v_ref[slot, 7 : 7 + NG], value, v_ref[slot, 9 : 9 + NG])


def silu_terms(half):
    t = jnp.tanh(half)
    product = half * t
    bump = 1.0 - t * t
    return half + product, (1.0 + t) + half * bump, bump * (1.0 - product)


def staggered(steps, groups):
    depth = len(steps)

    def turn(i, first, last):
        for n in reversed(range(first, last)):
            steps[n](i - n, 0)

    for i in range(depth - 1):
        turn(i, 0, i + 1)

    def body(i, carry):
        turn(i, 0, depth)
        return carry

    lax.fori_loop(depth - 1, groups, body, 0)
    for i in range(groups, groups + depth - 1):
        turn(i, i - groups + 1, depth)


def staggered_layer(steps, groups, layer, final):
    depth = len(steps)

    def turn(i, first):
        for n in reversed(range(first, depth)):
            group = jnp.maximum(i - n, 0)
            steps[n](lax.rem(group, groups), lax.div(group, groups))

    def body(i, carry):
        turn(layer * groups + i, 0)
        return carry

    lax.fori_loop(0, groups, body, 0)
    if final:
        for n in range(1, depth):
            turn(jnp.int32((layer + 1) * groups + n - 1), n)


def part(t):
    return slice(t * NG, (t + 1) * NG)


def first_stage(refs, u_refs, work, outs):
    w_ref, mix_ref = refs
    (u_ref,) = u_refs
    v_ref, left_ref = work[:2]
    h_ref, m_ref, a_ref, b_ref = outs
    wy, wx = taps_of(w_ref, 3, False), taps_of(w_ref, 6, False)
    bias = w_ref[ROW_BIAS1 : ROW_BIAS1 + 1, :]

    def taps(i, at):
        for t in range(GROUP):
            y = i * GROUP + t
            z = y + HALF
            top = along_y(wy, u_ref, jnp.bitwise_and(y + NG - 1, NG - 1), y, y + 1)
            end = along_y(wy, u_ref, z - 1, z, jnp.bitwise_and(z + 1, NG - 1))
            left_ref[part(t), :LANES] = along_x(wx, top, v_ref, 2 * t).astype(BF16)
            left_ref[part(t), LANES:] = along_x(wx, end, v_ref, 2 * t + 1).astype(BF16)

    def mix(i, at):
        mixed = jnp.dot(left_ref[...], mix_ref[...], preferred_element_type=F32)
        for t in range(GROUP):
            y = i * GROUP + t
            tangent = mixed[part(t), LANES:]
            value, slope, curve = silu_terms(mixed[part(t), :LANES] + bias)
            h_ref[at, y] = value.astype(BF16)
            m_ref[at, y] = (slope * tangent).astype(BF16)
            a_ref[at, y] = curve * tangent
            b_ref[at, y] = slope

    return taps, mix


def second_stage(refs, u_refs, work, outs):
    w_ref, mix_ref, back_ref = refs
    uh_ref, um_ref = u_refs
    v_ref, left_ref, next_ref = work
    rh_ref, rm_ref = outs
    wy, wx = taps_of(w_ref, 12, False), taps_of(w_ref, 15, False)
    bias = w_ref[ROW_BIAS2 : ROW_BIAS2 + 1, :]
    scale = w_ref[ROW_SCALE : ROW_SCALE + 1, :]

    def taps(i, at):
        for t in range(GROUP):
            y = i * GROUP + t
            sh = along_x(wx, along_y(wy, uh_ref, y, y + 1, y + 2), v_ref, 2 * t)
            sm = along_x(wx, along_y(wy, um_ref, y, y + 1, y + 2), v_ref, 2 * t + 1)
            left_ref[part(t), :LANES] = sh.astype(BF16)
            left_ref[part(t), LANES:] = sm.astype(BF16)

    def mix(i, at):
        mixed = jnp.dot(left_ref[...], mix_ref[...], preferred_element_type=F32)
        _, slope, curve = silu_terms(mixed[:, :LANES] + bias)
        next_ref[:, :LANES] = (slope * (0.5 * scale)).astype(BF16)
        next_ref[:, LANES:] = (curve * scale * mixed[:, LANES:]).astype(BF16)

    def back(i, at):
        mixed = jnp.dot(next_ref[...], back_ref[...], preferred_element_type=F32).astype(BF16)
        for t in range(GROUP):
            rh_ref[at, i * GROUP + t] = mixed[part(t), :LANES]
            rm_ref[at, i * GROUP + t] = mixed[part(t), LANES:]

    return taps, mix, back


def third_stage(refs, u_refs, work, outs):
    w_ref, back_ref, a_ref, b_ref = refs
    uh_ref, um_ref = u_refs
    v_ref, left_ref = work[:2]
    (y_ref,) = outs
    wy, wx = taps_of(w_ref, 12, True), taps_of(w_ref, 15, True)
    wx_half = taps_of(w_ref, ROW_HALF, True)

    def taps(i, at):
        for t in range(GROUP):
            y = i * GROUP + t
            g = along_x(wx, along_y(wy, uh_ref, y, y + 1, y + 2), v_ref, 2 * t)
            dg = along_x(wx_half, along_y(wy, um_ref, y, y + 1, y + 2), v_ref, 2 * t + 1)
            left_ref[part(t), :LANES] = (a_ref[at, y] * g + b_ref[at, y] * dg).astype(BF16)

    def back(i, at):
        mixed = jnp.dot(left_ref[:, :LANES], back_ref[...], preferred_element_type=F32)
        for t in range(GROUP):
            y_ref[at, i * GROUP + t] = mixed[part(t)].astype(BF16)

    return taps, back


def fourth_stage(refs, u_refs, work, outs):
    (w_ref,) = refs
    (u_ref,) = u_refs
    v_ref = work[0]
    (f_ref,) = outs
    wy, wx = taps_of(w_ref, 3, True), taps_of(w_ref, 6, True)

    def taps(i, at):
        for t in range(GROUP):
            y = i * GROUP + t
            out = along_x(wx, along_y(wy, u_ref, y, y + 1, y + 2), v_ref, t)
            f_ref[at, y] = out.astype(BF16).astype(F32)

    return (taps,)


STAGES = {
    "first": (first_stage, NG, (BF16, BF16, F32, F32), (0, 1), (0, False)),
    "second": (second_stage, HALF, (BF16, BF16), (0, 1), (9, False)),
    "third": (third_stage, HALF, (BF16,), (0,), (9, True)),
    "fourth": (fourth_stage, HALF, (F32,), (), (0, True)),
}


def taker(refs):
    left = list(refs)

    def take(n):
        got = left[:n]
        del left[:n]
        return got

    return take


def inner_kernel(stage, n_const, n_field, n_local, *refs):
    body, rows, kinds, _, (start, flip) = STAGES[stage]
    take = taker(refs)
    consts = take(n_const)
    fields = [take(3) for _ in range(n_field)]
    local, outs = take(n_local), take(len(kinds))
    u_refs, ring_refs = take(n_field), take(n_field)
    work = take(3)
    offset = 0 if rows == NG else 1
    wz = taps_of(consts[0], start, flip)
    inner = fields[0][1].shape[0]
    if stage == "fourth":
        outs = [outs[0].at[pl.ds(1, inner)]]
    steps = body(consts + local, u_refs, work, outs)

    def layer(step, which, index, final):
        for field, u_ref, ring_ref in zip(fields, u_refs, ring_refs):
            along_z_ring(wz, (field[which], index), step, ring_ref, u_ref, rows, offset)
            if offset:
                wrap_halves(u_ref)
        staggered_layer(steps, HALF // GROUP, step - 2, final)

    def loop(step, carry):
        layer(step, 1, step - 1, False)
        return carry

    for (low_ref, mid_ref, _), ring_ref in zip(fields, ring_refs):
        keep_layer((low_ref, 0), 0, ring_ref, rows)
        keep_layer((mid_ref, 0), 1, ring_ref, rows)
    lax.fori_loop(2, inner + 1, loop, 0)
    layer(inner + 1, 2, 0, True)


def edge_kernel(stage, n_const, n_field, n_local, places, *refs):
    body, rows, kinds, _, (start, flip) = STAGES[stage]
    take = taker(refs)
    consts = take(n_const)
    fields = [take(3) for _ in range(n_field)]
    local, outs, u_refs = take(n_local), take(len(kinds)), take(n_field)
    work = take(3)
    offset = 0 if rows == NG else 1
    wz = taps_of(consts[0], start, flip)
    for field, u_ref in zip(fields, u_refs):
        along_z(wz, list(zip(field, places)), u_ref, rows, offset)
        if offset:
            wrap_halves(u_ref)
    staggered(body(consts + local, u_refs, work, outs), HALF // GROUP)


def field_scratch(stage, n_field, ring):
    rows = STAGES[stage][1]
    u_rows = NG if rows == NG else HALF + 2
    scratch = [pltpu.VMEM((u_rows, NG, LANES), F32)] * n_field
    if ring:
        scratch += [pltpu.VMEM((3, rows, NG, LANES), F32)] * n_field
    left = pltpu.VMEM((GROUP * NG, 2 * LANES), BF16)
    return scratch + [pltpu.VMEM((2 * GROUP, NG + 16, LANES), F32), left, left]


def call_stage(kernel, name, layers, mib, kinds, args, scratch):
    return pl.pallas_call(
        kernel,
        out_shape=[jax.ShapeDtypeStruct((layers, HALF, NG, LANES), k) for k in kinds],
        in_specs=[vmem()] * len(args),
        out_specs=[vmem()] * len(kinds),
        scratch_shapes=scratch,
        compiler_params=params(mib),
        cost_estimate=cost(layers * 4_000_000_000, layers * 6_000_000),
        name=name,
    )(*args)


def run_inner(stage, consts, fields, local):
    kernel = functools.partial(inner_kernel, stage, len(consts), len(fields), len(local))
    args = [*consts, *[ref for field in fields for ref in field], *[x[1] for x in local]]
    scratch = field_scratch(stage, len(fields), True)
    layers = fields[0][1].shape[0]
    if stage == "fourth":
        layers += 2
    return call_stage(kernel, stage + "_inner", layers, 16, STAGES[stage][2], args, scratch)


def run_edge(stage, consts, fields, local, halos, side):
    last = fields[0][1].shape[0] - 1
    around, places = [], (0, 0, 0) if side == 0 else (last, 0, 0)
    for (low, mid, high), (below, above) in zip(fields, halos):
        around += [below, low, mid] if side == 0 else [mid, high, above]
    kernel = functools.partial(
        edge_kernel, stage, len(consts), len(fields), len(local), places
    )
    args = [*consts, *around, *[x[2 * side] for x in local]]
    scratch = field_scratch(stage, len(fields), False)
    name = stage + ("_low", "_high")[side]
    return call_stage(kernel, name, 1, 8, STAGES[stage][2], args, scratch)


def exchange(fields):
    size = lax.axis_size("slab")
    up = [(i, (i + 1) % size) for i in range(size)]
    down = [(j, i) for i, j in up]
    return [
        (lax.ppermute(high, "slab", up), lax.ppermute(low, "slab", down))
        for low, _, high in fields
    ]


def ends_kernel(w_ref, below_ref, low_ref, mid_ref, high_ref, above_ref, _, f_ref, *scratch):
    u_ref, *work = scratch
    inner = mid_ref.shape[0]
    wz = taps_of(w_ref, 0, True)
    for at, around in (
        (0, ((below_ref, 0), (low_ref, 0), (mid_ref, 0))),
        (inner + 1, ((mid_ref, inner - 1), (high_ref, 0), (above_ref, 0))),
    ):
        along_z(wz, around, u_ref, HALF, 1)
        wrap_halves(u_ref)
        out = [f_ref.at[pl.ds(at, 1)]]
        staggered(fourth_stage((w_ref,), (u_ref,), work, out), HALF // GROUP)


def run_ends(lanes, y, halos, field):
    low, mid, high = y
    below, above = halos
    return pl.pallas_call(
        ends_kernel,
        out_shape=jax.ShapeDtypeStruct(field.shape, F32),
        in_specs=[vmem()] * 7,
        out_specs=vmem(),
        scratch_shapes=field_scratch("fourth", 1, False),
        input_output_aliases={6: 0},
        compiler_params=params(8),
        name="ends",
    )(lanes, below, low, mid, high, above, field)


def gather_kernel(spots_ref, half_ref, f_ref, out_ref, rows_ref):
    count = rows_ref.shape[0]
    unroll = 128
    eye = jnp.where(
        lax.broadcasted_iota(jnp.int32, (LANES, LANES), 0)
        == lax.broadcasted_iota(jnp.int32, (LANES, LANES), 1),
        1.0,
        0.0,
    ).astype(BF16)

    def pick(i, carry):
        for t in range(unroll):
            atom = i * unroll + t
            rows_ref[pl.ds(atom, 1), :] = f_ref[pl.ds(spots_ref[atom], 1), :]
        return carry

    lax.fori_loop(0, count // unroll, pick, 0)
    width = min(BLOCK, count)
    for start in range(0, count, width):
        at = slice(start, start + width)
        turned = lax.dot_general(
            eye,
            rows_ref[at, :].astype(BF16),
            (((1,), (1,)), ((), ())),
            preferred_element_type=F32,
        )
        later = jnp.broadcast_to(half_ref[:, at], (CH, width)) == 1
        out_ref[:, at] = jnp.where(later, turned[CH:], turned[:CH]).astype(BF16)


def make_gather(spots, half, field):
    count = spots.shape[0]
    return pl.pallas_call(
        gather_kernel,
        out_shape=jax.ShapeDtypeStruct((CH, count), BF16),
        in_specs=[smem(), vmem(), vmem()],
        out_specs=vmem(),
        scratch_shapes=[pltpu.VMEM((count, LANES), F32)],
        compiler_params=params(6),
        cost_estimate=cost(500_000_000, 600_000),
        name="gather",
    )(spots, half.reshape(1, count), field)


def finish_kernel(peers, me_ref, tab_ref, *refs):
    out_ref, rows_ref, sems = refs[-3:]
    copies = []
    for n in range(peers):
        k = lax.rem(lax.bitwise_xor(me_ref[0], n), NT)
        rows_ref[n] = refs[n][...].astype(F32) * tab_ref[...]
        copies.append(pltpu.make_async_copy(rows_ref.at[n], out_ref.at[k], sems.at[n]))
        copies[-1].start()
    for copy in copies:
        copy.wait()


def make_output(me, tab, returned):
    count = len(returned)
    return pl.pallas_call(
        functools.partial(finish_kernel, count),
        out_shape=jax.ShapeDtypeStruct((NT,) + tab.shape, F32),
        in_specs=[smem()] + [vmem()] * (count + 1),
        out_specs=pl.BlockSpec(memory_space=pl.ANY),
        scratch_shapes=[
            pltpu.VMEM((count,) + tab.shape, F32),
            pltpu.SemaphoreType.DMA((count,)),
        ],
        compiler_params=params(8),
        name="finish",
    )(me, tab, *returned)


def swap(array, j):
    if j == 0:
        return array
    size = lax.axis_size("brick")
    return lax.ppermute(array, "brick", [(i, i ^ j) for i in range(size)])


def shards(
    features,
    tangents,
    route,
    cell_local,
    stencil,
    stencil_table,
    taps1,
    taps2,
    point1,
    point2,
    bias1,
    bias2,
    readout,
):
    bricks = lax.axis_size("brick")
    depth = NG // lax.axis_size("slab")
    me = lax.axis_index("brick").astype(jnp.int32)
    mine = me.reshape(1)

    tab, cell, *blocks = make_deposits(
        mine, features, tangents, stencil, stencil_table, route, cell_local, bricks
    )
    cell = cell.reshape(-1)
    chunks, cells = [blocks[0]], [cell]
    for j in range(1, bricks):
        block = blocks[j]
        if j == 3:
            (sums,) = run_scatter(first_sums_kernel, "own_sums", cells[:1], chunks[:1], None, depth)
            sums, point1 = lax.optimization_barrier((sums, point1))
        if j >= 3:
            sums, cell, block = lax.optimization_barrier((sums, cell, block))
        cells.append(swap(cell, j))
        chunks.append(swap(block, j))
    mix1, mix2, back2, back1, lanes = make_weights(
        point1, point2, taps1, taps2, bias1, bias2, readout
    )
    (sums,) = run_scatter(more_sums_kernel, "more_sums", cells[1:-1], chunks[1:-1], sums, depth)
    sums, low, high = run_scatter(charge_kernel, "charge", cells[-1:], chunks[-1:], sums, depth)
    charge = (low, inner_charge(sums, depth), high)

    def both(stage, consts, fields, local, halos):
        middle = run_inner(stage, consts, fields, local)
        lows = run_edge(stage, consts, fields, local, halos, 0)
        highs = run_edge(stage, consts, fields, local, halos, 1)
        return list(zip(lows, middle, highs))

    h, m, bend, slope = both("first", [lanes, mix1], [charge], [], exchange([charge]))
    rh, rm = both("second", [lanes, mix2, back2], [h, m], [], exchange([h, m]))
    (y,) = both("third", [lanes, back1], [rh, rm], [bend, slope], exchange([rh, rm]))
    ((below, above),) = exchange([y])
    (inner,) = run_inner("fourth", [lanes], [y], [])

    field = run_ends(lanes, y, (below, above), inner).reshape(-1, LANES)
    returned = [None] * NT
    for j in (*range(NT - 1, 0, -1), 0):
        y_of = (cells[j] // NG) % NG
        spots = ((cells[j] // (NG * NG)) * HALF + y_of % HALF) * NG + cells[j] % NG
        returned[j] = swap(make_gather(spots, y_of // HALF, field), j)
    return make_output(mine, tab, returned)


def solution(mesh):
    placed = (
        P(None, ("slab", "brick")),
        P(None, None, ("slab", "brick")),
        P(("slab", "brick"), None),
        P(("slab", "brick")),
        P(("slab", "brick")),
        P(),
        P(),
        P(),
        P(),
        P(),
        P(),
        P(),
        P(),
    )
    return jax.shard_map(
        shards,
        mesh=mesh,
        in_specs=placed,
        out_specs=P(None, None, ("slab", "brick")),
        check_vma=False,
    )
```
